1024 devices in a mesh: replica: 64 (over y_hi, x, core), tensor: 16 (over z, y_lo).
Axes of the slice: x: 8, y: 8 (y_hi: 4, y_lo: 2; y = y_hi * 2 + y_lo), z: 8, core: 2. Of those that a mesh axis runs over, the one named last changes fastest.
Arguments:
- hidden_rows: bfloat16 [512, 8, 8192], P('replica'), may hold values from -6 to 6
- prior_bias: bfloat16 [2048], P('tensor'), may hold values from -4 to 4
- cache_blocks: bfloat16 [16, 256, 1024, 256], P('tensor', 'replica'), may hold values from -5 to 5
- queries: bfloat16 [16, 256, 8, 1024], P('tensor', 'replica'), may hold values from -125 to 125
- cache_lengths: int32 [512], P('replica'), may hold values from 2 to 1024, as said below
- updated_rows: bfloat16 [8192, 2048], P(('replica', 'tensor')), may hold values from -0.0625 to 0.0625
Outputs:
- attended: bfloat16 [16, 256, 8, 1024], P('tensor', 'replica')
- updated_columns: bfloat16 [8192, 2048], P(None, 'tensor')
The draws below stay inside these ranges and needn't reach their ends.
Inputs may be any that keep to these rules, and one draw needn't show every extreme that they name: `cache_lengths`: each row's length lies between 2 and 1024; some row has exactly 1024.
All inputs are finite; a program needn't handle non-finite values.
Results may differ from the reference program's by a relative error of at most 0.0065.
Values may be sent and summed in bfloat16 or wider, within the bound.
A program may use at most 32 MiB of HBM per device.

```python
import math
import jax
import jax.numpy as jnp
from jax import lax

D = 8192
HD = 128
GROUP = 8
KVH = 8
STEPS = 8
ROWS = 8
LMAX = 1024
ROWS_ALL = 512
SLOT_ROWS = 256
COLS = 2048
N_REPLICA = 64


def draw_cache_blocks(key, part):
    key = jax.random.fold_in(key, 3)
    values = jnp.clip(jax.random.normal(key, (2 * KVH, SLOT_ROWS, LMAX, 2 * HD), jnp.float32), -4.0, 4.0)
    return values.astype(jnp.bfloat16)


def draw_queries(key, part):
    key = jax.random.fold_in(key, 5)
    values = jnp.clip(jax.random.normal(key, (2 * KVH, SLOT_ROWS, STEPS, GROUP, HD), jnp.float32), -4.0, 4.0)
    return values.reshape(2 * KVH, SLOT_ROWS, STEPS, GROUP * HD).astype(jnp.bfloat16)


def draw_cache_lengths(key, part):
    key = jax.random.fold_in(key, 7)
    lengths = jax.random.randint(jax.random.fold_in(key, 1), (ROWS_ALL,), 2, LMAX + 1)
    chosen = jax.random.randint(jax.random.fold_in(key, 2), (), 0, ROWS_ALL)
    return lengths.at[chosen].set(LMAX).astype(jnp.int32)


def block_levels(rng, dims, split, smallest, high):
    factor_of = 1.0
    for dim, parts in split:
        steps = jax.random.uniform(jax.random.fold_in(jax.random.fold_in(rng, 6), dim), (parts,), jnp.float32, smallest / len(split), high / len(split))
        factor_of = factor_of * jnp.repeat(jnp.exp(steps), dims[dim] // parts).reshape((-1,) + (1,) * (len(dims) - 1 - dim))
    return factor_of


def scatter_about(own_key, shape, width, most, pieces=(), kind=jnp.bfloat16):
    values = width * jax.random.normal(own_key, shape, jnp.float32)
    if pieces:
        values = values * block_levels(own_key, shape, pieces, -0.22, 0.18)
    return jnp.clip(values, -most, most).astype(kind)


def setup_inputs(seed: int = 0) -> dict:
    splits = jax.random.split(jax.random.key(seed), 7)
    hidden_rows = scatter_about(splits[0], (ROWS_ALL, STEPS, D), 1.0, 6.0, ((0, 64),))
    prior_bias = scatter_about(splits[1], (COLS,), 1.0, 4.0, ((0, 16),))
    cache_blocks = draw_cache_blocks(jax.random.fold_in(splits[6], 71), 0)
    queries = draw_queries(jax.random.fold_in(splits[6], 71), 0)
    cache_lengths = draw_cache_lengths(jax.random.fold_in(splits[6], 71), 0)
    updated_rows = scatter_about(splits[5], (D, COLS), D ** -0.5, 0.0625, ((0, 1024),))
    return dict(hidden_rows=hidden_rows, prior_bias=prior_bias, cache_blocks=cache_blocks, queries=queries, cache_lengths=cache_lengths, updated_rows=updated_rows)


rope_base = 1000000.0

def rotate_keys(vectors, positions):
    extent = vectors.shape[-1]
    middle = extent // 2
    frequency = jnp.exp(jnp.arange(middle, dtype=jnp.float32) * (-2.0 * math.log(rope_base) / extent))
    angles = positions.astype(jnp.float32)[..., None] * frequency
    cos_part = jnp.concatenate([jnp.cos(angles), jnp.cos(angles)], axis=-1)
    sine_part = jnp.concatenate([jnp.sin(angles), jnp.sin(angles)], axis=-1)
    turned = jnp.concatenate([-vectors[..., middle:], vectors[..., :middle]], axis=-1)
    return vectors * cos_part + turned * sine_part

def attend(query_rows, cache_rows, new_keys, new_values, row_lengths):
    row_count, step_count, query_width = query_rows.shape
    extent = new_keys.shape[-1]
    groups = query_width // extent
    query_heads = query_rows.reshape(row_count, step_count, groups, extent).astype(jnp.float32)
    cached_keys = cache_rows[:, :, :extent].astype(jnp.float32)
    cached_values = cache_rows[:, :, extent:].astype(jnp.float32)
    score_scale = 1.0 / math.sqrt(extent)
    old_scores = jnp.einsum('rsgd,rpd->rsgp', query_heads, cached_keys) * score_scale
    fresh_scores = jnp.einsum('rsgd,rud->rsgu', query_heads, new_keys.astype(jnp.float32)) * score_scale
    places = jnp.arange(cache_rows.shape[1], dtype=jnp.int32)
    old_valid = places[None, :] < row_lengths[:, None]
    old_scores = jnp.where(old_valid[:, None, None, :], old_scores, -1e+30)
    steps_range = jnp.arange(step_count, dtype=jnp.int32)
    causal = steps_range[None, :] <= steps_range[:, None]
    fresh_scores = jnp.where(causal[None, :, None, :], fresh_scores, -1e+30)
    peak_score = jnp.maximum(lax.optimization_barrier(jnp.max(old_scores, axis=-1)), lax.optimization_barrier(jnp.max(fresh_scores, axis=-1)))[..., None]
    old_exp = jnp.exp(old_scores - peak_score)
    fresh_exp = jnp.exp(fresh_scores - peak_score)
    denominator = lax.optimization_barrier(jnp.sum(old_exp, axis=-1, keepdims=True)) + lax.optimization_barrier(jnp.sum(fresh_exp, axis=-1, keepdims=True))
    old_weights = (old_exp / denominator).astype(jnp.bfloat16).astype(jnp.float32)
    fresh_weights = (fresh_exp / denominator).astype(jnp.bfloat16).astype(jnp.float32)
    output = jnp.einsum('rsgp,rpd->rsgd', old_weights, cached_values)
    output = output + jnp.einsum('rsgu,rud->rsgd', fresh_weights, new_values.astype(jnp.float32))
    return output.reshape(row_count, step_count, query_width).astype(jnp.bfloat16)

def to_slots(array):
    parted = array.reshape(N_REPLICA, 2, ROWS // 2, STEPS, KVH, HD)
    parted = jnp.transpose(parted, (4, 1, 0, 2, 3, 5))
    return parted.reshape(2 * KVH, SLOT_ROWS, STEPS, HD)

def reference(hidden_rows, prior_bias, cache_blocks, queries, cache_lengths, updated_rows):
    flattened = hidden_rows.reshape(ROWS_ALL * STEPS, D)
    projected = jnp.dot(flattened, updated_rows, preferred_element_type=jnp.float32) + prior_bias.astype(jnp.float32)
    projected = projected.reshape(ROWS_ALL, STEPS, KVH, 2, HD)
    positions = cache_lengths[:, None] + jnp.arange(STEPS, dtype=jnp.int32)[None, :]
    new_keys = rotate_keys(projected[:, :, :, 0, :], positions[:, :, None]).astype(jnp.bfloat16)
    new_values = projected[:, :, :, 1, :].astype(jnp.bfloat16)
    key_slots = to_slots(new_keys)
    value_slots = to_slots(new_values)
    length_rows = jnp.transpose(cache_lengths.reshape(N_REPLICA, 2, ROWS // 2), (1, 0, 2)).reshape(2, SLOT_ROWS)
    length_slots = jnp.broadcast_to(length_rows[None], (KVH, 2, SLOT_ROWS)).reshape(2 * KVH, SLOT_ROWS)

    def one_slot(items):
        return attend(items[0], items[1], items[2], items[3], items[4])
    attended = lax.map(one_slot, (queries, cache_blocks, key_slots, value_slots, length_slots))
    return (attended, updated_rows)
```

```python
import functools
import math

import jax
import jax.numpy as jnp
from jax import lax
from jax.experimental import pallas as pl
from jax.experimental.pallas import tpu as pltpu
from jax.sharding import PartitionSpec as P

ROPE_BASE = 1000000.0
HD = 128
NEG = -1e30
MESH = pl.DeviceIdType.MESH
NT = (((1,), (1,)), ((), ()))


def kernel(
    NY, NX, NTEN, PIECE, STEPS,
    rows_hbm, hidden_hbm, cache_hbm, query_hbm, bias_ref, len_ref,
    cols, att,
    parts, hidden, cache, query, mine, other,
    part_send, part_recv, send, recv, load, pair_send, pair_recv,
):
    rep = lax.axis_index("replica")
    ten = lax.axis_index("tensor")
    core = lax.rem(rep, 2)
    chip = lax.div(rep, 2)
    x = lax.rem(chip, NX)
    y = lax.div(chip, NX)
    parity = lax.rem(ten, 2)
    block = NTEN * PIECE

    def replica(dy, dx, c=None):
        yy = lax.rem(y + dy + 2 * NY, NY)
        xx = lax.rem(x + dx + 2 * NX, NX)
        return (yy * NX + xx) * 2 + (core if c is None else c)

    right, left = replica(0, 1), replica(0, -1)
    sibling = replica(0, 0, 1 - core)
    ahead = [replica(d, 0) for d in range(1, NY)]
    peers = [lax.rem(ten + k, NTEN) for k in range(1, NTEN)]

    barrier = pltpu.get_barrier_semaphore()
    for p in peers:
        pl.semaphore_signal(barrier, inc=1, device_id=(rep, p), device_id_type=MESH)
    for r in [right, left, sibling, *ahead]:
        pl.semaphore_signal(barrier, inc=1, device_id=(r, ten), device_id_type=MESH)

    loads = [
        pltpu.make_async_copy(query_hbm, query, load.at[0]),
        pltpu.make_async_copy(cache_hbm, cache, load.at[1]),
        pltpu.make_async_copy(hidden_hbm, hidden, load.at[2]),
        pltpu.make_async_copy(
            rows_hbm.at[:, pl.ds(pl.multiple_of(ten * HD, HD), HD)], parts.at[0], load.at[3]
        ),
    ]
    loads[3].start()
    for c in loads[:3]:
        c.start()
    pl.semaphore_wait(barrier, len(peers) + 3 + len(ahead))

    for k, p in enumerate(peers, 1):
        pltpu.make_async_remote_copy(
            src_ref=rows_hbm.at[:, pl.ds(pl.multiple_of(p * HD, HD), HD)],
            dst_ref=parts.at[k],
            send_sem=part_send,
            recv_sem=part_recv,
            device_id=(rep, p),
            device_id_type=MESH,
        ).start()

    def at(r):
        return cols.at[pl.ds(pl.multiple_of(r * block, block), block), :]

    def push(r, to):
        pltpu.make_async_remote_copy(
            src_ref=at(r), dst_ref=at(r), send_sem=send, recv_sem=recv.at[r],
            device_id=(to, ten), device_id_type=MESH,
        ).start()

    def arrived(r):
        pltpu.make_async_copy(at(r), at(r), recv.at[r]).wait()

    lane = lax.broadcasted_iota(jnp.int32, (1, HD), 1)
    half = lax.rem(lane, HD // 2).astype(jnp.float32)
    frequency = jnp.exp(half * (-2.0 * math.log(ROPE_BASE) / HD))
    step = lax.broadcasted_iota(jnp.int32, (STEPS, HD), 0)
    n_rows = hidden.shape[0] // STEPS
    position = jnp.concatenate([step + len_ref[b] for b in range(n_rows)], axis=0)
    angle = position.astype(jnp.float32) * frequency
    cosine = jnp.cos(angle)
    sine = jnp.sin(angle) * jnp.where(lane < HD // 2, -1.0, 1.0)

    scale = 1.0 / math.sqrt(HD)
    n_att = query.shape[0]
    groups = query.shape[2] // HD
    queries, peaks, totals, sums = [], [], [], []

    def attend_cached(i):
        if i == 0:
            loads[0].wait()
            loads[1].wait()
        wide = query[i].astype(jnp.float32)
        q = jnp.concatenate([wide[:, g * HD : (g + 1) * HD] for g in range(groups)], axis=0)
        q = q.astype(jnp.bfloat16)
        s = lax.dot_general(q, cache[i, :, :HD], NT, preferred_element_type=jnp.float32) * scale
        place = lax.broadcasted_iota(jnp.int32, s.shape, 1)
        s = jnp.where(place < len_ref[parity * n_att + i], s, NEG)
        m = jnp.max(s, axis=1, keepdims=True)
        e = jnp.exp(s - m)
        queries.append(q)
        peaks.append(m)
        totals.append(jnp.sum(e, axis=1, keepdims=True))
        sums.append(
            jnp.dot(e.astype(jnp.bfloat16), cache[i, :, HD:], preferred_element_type=jnp.float32)
        )

    projected = [jnp.zeros((hidden.shape[0], HD), jnp.float32)]

    def project(dy, dx):
        c = lax.div(replica(dy, dx), 2)
        span = pl.ds(pl.multiple_of(c * 2 * block, 2 * block), 2 * block)
        projected[0] += jnp.dot(hidden[:, span], cols[span, :], preferred_element_type=jnp.float32)

    attend_cached(0)

    loads[3].wait()
    pltpu.make_async_copy(parts.at[pl.ds(1, NTEN - 1)], parts.at[pl.ds(1, NTEN - 1)], part_recv).wait()
    pieces = [
        parts[lax.rem(ten - k + NTEN, NTEN)].astype(jnp.float32) for k in range(NTEN)
    ]
    cols[pl.ds(pl.multiple_of(rep * block, block), block), :] = jnp.concatenate(
        pieces, axis=0
    ).astype(jnp.bfloat16)

    push(rep, right)
    push(rep, left)
    for r in ahead:
        push(rep, r)
    push(rep, sibling)

    attend_cached(1)
    order = [d for d in (1, NY - 1, 2) if d < NY] if NY > 2 else list(range(1, NY))
    for d in order:
        r = replica(d, 0)
        arrived(r)
        push(r, right)
        push(r, left)
        push(r, sibling)

    waiting = [(d, 0) for d in [0, *order]]
    cached_left = list(range(2, n_att))
    loads[2].wait()
    for s in range(1, NX // 2 + 1):
        fresh = []
        for j, d in enumerate([0, *order]):
            to_right = NX // 2 if j % 2 == 0 else NX // 2 - 1
            to_left = NX - 1 - to_right
            if s <= to_right:
                r = replica(d, -s)
                arrived(r)
                if s < to_right:
                    push(r, right)
                push(r, sibling)
                fresh.append((d, -s))
            if s <= to_left:
                r = replica(d, s)
                arrived(r)
                if s < to_left:
                    push(r, left)
                push(r, sibling)
                fresh.append((d, s))
        if cached_left:
            attend_cached(cached_left.pop(0))
        for dy, dx in waiting:
            arrived(replica(dy, dx, 1 - core))
            project(dy, dx)
        waiting = fresh
    for i in cached_left:
        attend_cached(i)
    for dy, dx in waiting:
        arrived(replica(dy, dx, 1 - core))
        project(dy, dx)

    whole = projected[0] + bias_ref[...].astype(jnp.float32)
    rotated = whole * cosine + pltpu.roll(whole, HD // 2, 1) * sine
    whole = jnp.where(parity == 0, rotated, whole).astype(jnp.bfloat16)
    n_half = whole.shape[0] // 2
    mine[0] = whole[:n_half]
    mine[1] = whole[n_half:]
    exchange = pltpu.make_async_remote_copy(
        src_ref=mine.at[1 - parity], dst_ref=other, send_sem=pair_send, recv_sem=pair_recv,
        device_id=(rep, ten + 1 - 2 * parity), device_id_type=MESH,
    )
    exchange.start()
    exchange.wait()
    kept, got = mine[parity], other[...]
    new_keys = jnp.where(parity == 0, kept, got)
    new_values = jnp.where(parity == 0, got, kept)

    q = jnp.concatenate(queries, axis=0)
    s = lax.dot_general(q, new_keys, NT, preferred_element_type=jnp.float32) * scale
    of_query = lax.broadcasted_iota(jnp.int32, s.shape, 0)
    of_key = lax.broadcasted_iota(jnp.int32, s.shape, 1)
    same_row = lax.div(of_query, groups * STEPS) == lax.div(of_key, STEPS)
    causal = lax.rem(of_key, STEPS) <= lax.rem(of_query, STEPS)
    s = jnp.where(same_row & causal, s, NEG)
    old_peak = jnp.concatenate(peaks, axis=0)
    peak = jnp.maximum(old_peak, jnp.max(s, axis=1, keepdims=True))
    e = jnp.exp(s - peak)
    shrink = jnp.exp(old_peak - peak)
    total = jnp.concatenate(totals, axis=0) * shrink + jnp.sum(e, axis=1, keepdims=True)
    out = jnp.concatenate(sums, axis=0) * shrink
    out += jnp.dot(e.astype(jnp.bfloat16), new_values, preferred_element_type=jnp.float32)
    out = out / total
    for i in range(n_att):
        base = i * groups * STEPS
        att[i] = jnp.concatenate(
            [out[base + g * STEPS : base + (g + 1) * STEPS] for g in range(groups)], axis=1
        ).astype(jnp.bfloat16)

    pltpu.make_async_copy(
        parts.at[pl.ds(1, NTEN - 1)], parts.at[pl.ds(1, NTEN - 1)], part_send
    ).wait()
    sent = cols.at[pl.ds(0, (2 * NY * NX - 1) * block), :]
    pltpu.make_async_copy(sent, sent, send).wait()


def solution(mesh):
    n_rep, n_ten = mesh.shape["replica"], mesh.shape["tensor"]
    NX = 8
    NY = n_rep // (2 * NX)

    def per_device(hidden_rows, prior_bias, cache_blocks, queries, cache_lengths, updated_rows):
        n_rows, steps, width = hidden_rows.shape
        piece = updated_rows.shape[0]
        any_space = pl.BlockSpec(memory_space=pl.ANY)
        vmem = pl.BlockSpec(memory_space=pltpu.VMEM)
        block = n_ten * piece
        attended, columns = pl.pallas_call(
            functools.partial(kernel, NY, NX, n_ten, piece, steps),
            out_shape=(
                jax.ShapeDtypeStruct((n_rep * block, HD), jnp.bfloat16),
                jax.ShapeDtypeStruct(queries.shape[1:], jnp.bfloat16),
            ),
            in_specs=[any_space] * 4 + [vmem, pl.BlockSpec(memory_space=pltpu.SMEM)],
            out_specs=(vmem, vmem),
            scratch_shapes=[
                pltpu.VMEM((n_ten, piece, HD), jnp.bfloat16),
                pltpu.VMEM((n_rows * steps, width), jnp.bfloat16),
                pltpu.VMEM(cache_blocks.shape[1:], jnp.bfloat16),
                pltpu.VMEM(queries.shape[1:], jnp.bfloat16),
                pltpu.VMEM((2, n_rows * steps // 2, HD), jnp.bfloat16),
                pltpu.VMEM((n_rows * steps // 2, HD), jnp.bfloat16),
                pltpu.SemaphoreType.DMA,
                pltpu.SemaphoreType.DMA,
                pltpu.SemaphoreType.DMA,
                pltpu.SemaphoreType.DMA((n_rep,)),
                pltpu.SemaphoreType.DMA((4,)),
                pltpu.SemaphoreType.DMA,
                pltpu.SemaphoreType.DMA,
            ],
            compiler_params=pltpu.CompilerParams(
                collective_id=0, has_side_effects=True, vmem_limit_bytes=40 << 20
            ),
        )(
            updated_rows,
            hidden_rows.reshape(n_rows * steps, width),
            cache_blocks[0],
            queries[0],
            prior_bias.reshape(1, HD),
            cache_lengths,
        )[::-1]
        return attended[None], columns

    return jax.shard_map(
        per_device,
        mesh=mesh,
        in_specs=(
            P("replica", None, None),
            P("tensor"),
            P("tensor", "replica", None, None),
            P("tensor", "replica", None, None),
            P("replica"),
            P(("replica", "tensor"), None),
        ),
        out_specs=(P("tensor", "replica", None, None), P(None, "tensor")),
        check_vma=False,
    )
```

```python
import functools
import math

import jax
import jax.numpy as jnp
from jax import lax
from jax.experimental import pallas as pl
from jax.experimental.pallas import tpu as pltpu
from jax.sharding import PartitionSpec as P

ROPE_BASE = 1000000.0
HD = 128
NEG = -1e30
MESH = pl.DeviceIdType.MESH
NT = (((1,), (1,)), ((), ()))


def kernel(
    NY, NX, NTEN, PIECE, STEPS,
    rows_hbm, hidden_hbm, cache_hbm, query_hbm, bias_hbm, len_hbm,
    cols, att,
    parts, hidden, cache, query, bias_ref, len_ref, mine, other,
    part_send, part_recv, send, recv, load, pair_send, pair_recv,
):
    rep = lax.axis_index("replica")
    ten = lax.axis_index("tensor")
    core = lax.rem(rep, 2)
    chip = lax.div(rep, 2)
    x = lax.rem(chip, NX)
    y = lax.div(chip, NX)
    parity = lax.rem(ten, 2)
    block = NTEN * PIECE

    def replica(dy, dx, c=None):
        yy = lax.rem(y + dy + 2 * NY, NY)
        xx = lax.rem(x + dx + 2 * NX, NX)
        return (yy * NX + xx) * 2 + (core if c is None else c)

    sibling = replica(0, 0, 1 - core)
    beside = {d: replica(0, d) for d in (1, -1, 2, -2)}
    ahead = [replica(d, 0) for d in range(1, NY)]
    layer = lax.div(ten, 2)

    barrier = pltpu.get_barrier_semaphore()
    for p in reversed(range(NTEN)):

        @pl.when((p >= 2 * layer) & (p != ten))
        def _():
            pl.semaphore_signal(barrier, inc=1, device_id=(rep, p), device_id_type=MESH)

    plane = [*beside.values(), *ahead, sibling]
    for r in plane:
        pl.semaphore_signal(barrier, inc=1, device_id=(r, ten), device_id_type=MESH)

    loads = [
        pltpu.make_async_copy(query_hbm, query, load.at[0]),
        pltpu.make_async_copy(cache_hbm, cache, load.at[1]),
        pltpu.make_async_copy(hidden_hbm, hidden, load.at[2]),
        pltpu.make_async_copy(
            rows_hbm.at[:, pl.ds(pl.multiple_of(ten * HD, HD), HD)], parts.at[ten], load.at[3]
        ),
        pltpu.make_async_copy(len_hbm, len_ref, load.at[4]),
        pltpu.make_async_copy(bias_hbm, bias_ref, load.at[5]),
    ]
    for i in (3, 4, 5, 0, 1, 2):
        loads[i].start()
    pl.semaphore_wait(barrier, len(plane) + 2 * layer + 1)

    def give(p):
        pltpu.make_async_remote_copy(
            src_ref=rows_hbm.at[:, pl.ds(p * HD, HD)], dst_ref=parts.at[ten],
            send_sem=part_send, recv_sem=part_recv.at[ten],
            device_id=(rep, p), device_id_type=MESH,
        ).start()

    def take(p):
        pltpu.make_async_copy(parts.at[p], parts.at[p], part_recv.at[p]).wait()

    for p in range(NTEN):

        @pl.when((p < 2 * layer + 2) & (p != ten))
        def _():
            give(p)

    def at(r):
        return cols.at[pl.ds(pl.multiple_of(r * block, block), block), :]

    def push(r, to):
        pltpu.make_async_remote_copy(
            src_ref=at(r), dst_ref=at(r), send_sem=send, recv_sem=recv.at[r],
            device_id=(to, ten), device_id_type=MESH,
        ).start()

    def arrived(r):
        pltpu.make_async_copy(at(r), at(r), recv.at[r]).wait()

    lane = lax.broadcasted_iota(jnp.int32, (1, HD), 1)
    half = lax.rem(lane, HD // 2).astype(jnp.float32)
    frequency = jnp.exp(half * (-2.0 * math.log(ROPE_BASE) / HD))
    step = lax.broadcasted_iota(jnp.int32, (STEPS, HD), 0)
    n_rows = hidden.shape[0] // STEPS
    loads[4].wait()
    position = jnp.concatenate([step + len_ref[b] for b in range(n_rows)], axis=0)
    angle = position.astype(jnp.float32) * frequency
    cosine = jnp.cos(angle)
    sine = jnp.sin(angle) * jnp.where(lane < HD // 2, -1.0, 1.0)

    scale = 1.0 / math.sqrt(HD)
    n_att = query.shape[0]
    groups = query.shape[2] // HD
    queries, peaks, totals, sums = [], [], [], []

    def attend_cached(i):
        if i == 0:
            loads[0].wait()
            loads[1].wait()
        wide = query[i].astype(jnp.float32)
        q = jnp.concatenate([wide[:, g * HD : (g + 1) * HD] for g in range(groups)], axis=0)
        q = q.astype(jnp.bfloat16)
        s = lax.dot_general(q, cache[i, :, :HD], NT, preferred_element_type=jnp.float32) * scale
        place = lax.broadcasted_iota(jnp.int32, s.shape, 1)
        s = jnp.where(place < len_ref[parity * n_att + i], s, NEG)
        m = jnp.max(s, axis=1, keepdims=True)
        e = jnp.exp(s - m)
        queries.append(q)
        peaks.append(m)
        totals.append(jnp.sum(e, axis=1, keepdims=True))
        sums.append(
            jnp.dot(e.astype(jnp.bfloat16), cache[i, :, HD:], preferred_element_type=jnp.float32)
        )

    projected = [jnp.zeros((hidden.shape[0], HD), jnp.float32)]

    def project(dy, dx):
        c = lax.div(replica(dy, dx), 2)
        span = pl.ds(pl.multiple_of(c * 2 * block, 2 * block), 2 * block)
        projected[0] += jnp.dot(hidden[:, span], cols[span, :], preferred_element_type=jnp.float32)

    for i in range(n_att):
        attend_cached(i)
    loads[2].wait()

    for p in range(2, NTEN, 2):

        @pl.when(p > 2 * layer)
        def _():
            take(p)
            take(p + 1)
            give(p)
            give(p + 1)

    for p in range(NTEN):

        @pl.when((p < 2 * layer + 2) & (p != ten))
        def _():
            take(p)

    loads[3].wait()
    pieces = [parts[p].astype(jnp.float32) for p in range(NTEN)]
    cols[pl.ds(pl.multiple_of(rep * block, block), block), :] = jnp.concatenate(
        pieces, axis=0
    ).astype(jnp.bfloat16)

    def spread(dy):
        r = replica(dy, 0)
        for d in (2, -2, 1, -1):
            push(r, beside[d])
        push(r, sibling)

    def onward(dy, far):
        for d in (2, -2):
            r = replica(dy, -d)
            arrived(r)
            if far == d:
                push(r, beside[d])
            push(r, beside[d // 2])
            push(r, sibling)

    def handed(dy, d):
        r = replica(dy, -d)
        arrived(r)
        push(r, sibling)

    def both(dy, dx):
        arrived(replica(dy, dx, 1 - core))
        project(dy, dx)

    for r in ahead:
        push(rep, r)
    spread(0)
    ys = [d for d in (1, NY - 1, 2)][: NY - 1]
    fars = {d: (2, -2)[i % 2] for i, d in enumerate([0, *ys])}
    onward(0, fars[0])
    for d in ys:
        arrived(replica(d, 0))
        spread(d)
    handed(0, 1)
    handed(0, -1)
    both(0, 0)
    for dy in ys:
        onward(dy, fars[dy])
    for dx in (1, -1, 2, -2):
        both(0, dx)
    for dy in ys:
        handed(dy, 1)
        handed(dy, -1)
    for dy in ys:
        both(dy, 0)
    for dy in [0, *ys]:
        for d in (3, -3, 4):
            handed(dy, d)
        if dy != 0:
            for dx in (1, -1, 2, -2):
                both(dy, dx)
    for dy in [0, *ys]:
        for dx in (3, -3, 4):
            both(dy, dx)

    loads[5].wait()
    whole = projected[0] + bias_ref[...].astype(jnp.float32)
    rotated = whole * cosine + pltpu.roll(whole, HD // 2, 1) * sine
    whole = jnp.where(parity == 0, rotated, whole).astype(jnp.bfloat16)
    n_half = whole.shape[0] // 2
    mine[0] = whole[:n_half]
    mine[1] = whole[n_half:]
    exchange = pltpu.make_async_remote_copy(
        src_ref=mine.at[1 - parity], dst_ref=other, send_sem=pair_send, recv_sem=pair_recv,
        device_id=(rep, ten + 1 - 2 * parity), device_id_type=MESH,
    )
    exchange.start()
    exchange.wait()
    kept, got = mine[parity], other[...]
    new_keys = jnp.where(parity == 0, kept, got)
    new_values = jnp.where(parity == 0, got, kept)

    q = jnp.concatenate(queries, axis=0)
    s = lax.dot_general(q, new_keys, NT, preferred_element_type=jnp.float32) * scale
    of_query = lax.broadcasted_iota(jnp.int32, s.shape, 0)
    of_key = lax.broadcasted_iota(jnp.int32, s.shape, 1)
    same_row = lax.div(of_query, groups * STEPS) == lax.div(of_key, STEPS)
    causal = lax.rem(of_key, STEPS) <= lax.rem(of_query, STEPS)
    s = jnp.where(same_row & causal, s, NEG)
    old_peak = jnp.concatenate(peaks, axis=0)
    peak = jnp.maximum(old_peak, jnp.max(s, axis=1, keepdims=True))
    e = jnp.exp(s - peak)
    shrink = jnp.exp(old_peak - peak)
    total = jnp.concatenate(totals, axis=0) * shrink + jnp.sum(e, axis=1, keepdims=True)
    out = jnp.concatenate(sums, axis=0) * shrink
    out += jnp.dot(e.astype(jnp.bfloat16), new_values, preferred_element_type=jnp.float32)
    out = out / total
    for i in range(n_att):
        base = i * groups * STEPS
        att[i] = jnp.concatenate(
            [out[base + g * STEPS : base + (g + 1) * STEPS] for g in range(groups)], axis=1
        ).astype(jnp.bfloat16)

    given = parts.at[pl.ds(0, NTEN - 1)]
    pltpu.make_async_copy(given, given, part_send).wait()
    sent = cols.at[pl.ds(0, (2 * NY * NX - 1) * block), :]
    pltpu.make_async_copy(sent, sent, send).wait()


def solution(mesh):
    n_rep, n_ten = mesh.shape["replica"], mesh.shape["tensor"]
    NX = 8
    NY = n_rep // (2 * NX)

    def per_device(hidden_rows, prior_bias, cache_blocks, queries, cache_lengths, updated_rows):
        n_rows, steps, width = hidden_rows.shape
        piece = updated_rows.shape[0]
        vmem = pl.BlockSpec(memory_space=pltpu.VMEM)
        block = n_ten * piece
        attended, columns = pl.pallas_call(
            functools.partial(kernel, NY, NX, n_ten, piece, steps),
            out_shape=(
                jax.ShapeDtypeStruct((n_rep * block, HD), jnp.bfloat16),
                jax.ShapeDtypeStruct(queries.shape[1:], jnp.bfloat16),
            ),
            in_specs=[pl.BlockSpec(memory_space=pltpu.HBM)] * 6,
            out_specs=(vmem, vmem),
            scratch_shapes=[
                pltpu.VMEM((n_ten, piece, HD), jnp.bfloat16),
                pltpu.VMEM((n_rows * steps, width), jnp.bfloat16),
                pltpu.VMEM(cache_blocks.shape[1:], jnp.bfloat16),
                pltpu.VMEM(queries.shape[1:], jnp.bfloat16),
                pltpu.VMEM((1, HD), jnp.bfloat16),
                pltpu.SMEM((n_rows,), jnp.int32),
                pltpu.VMEM((2, n_rows * steps // 2, HD), jnp.bfloat16),
                pltpu.VMEM((n_rows * steps // 2, HD), jnp.bfloat16),
                pltpu.SemaphoreType.DMA,
                pltpu.SemaphoreType.DMA((n_ten,)),
                pltpu.SemaphoreType.DMA,
                pltpu.SemaphoreType.DMA((n_rep,)),
                pltpu.SemaphoreType.DMA((6,)),
                pltpu.SemaphoreType.DMA,
                pltpu.SemaphoreType.DMA,
            ],
            compiler_params=pltpu.CompilerParams(
                collective_id=0, has_side_effects=True, vmem_limit_bytes=40 << 20
            ),
        )(
            *(
                pltpu.with_memory_space_constraint(a, pltpu.HBM)
                for a in (
                    updated_rows,
                    hidden_rows.reshape(n_rows * steps, width),
                    cache_blocks[0],
                    queries[0],
                    prior_bias.reshape(1, HD),
                    cache_lengths,
                )
            )
        )[::-1]
        return attended[None], columns

    return jax.shard_map(
        per_device,
        mesh=mesh,
        in_specs=(
            P("replica", None, None),
            P("tensor"),
            P("tensor", "replica", None, None),
            P("tensor", "replica", None, None),
            P("replica"),
            P(("replica", "tensor"), None),
        ),
        out_specs=(P("tensor", "replica", None, None), P(None, "tensor")),
        check_vma=False,
    )
```

```python
import functools
import math

import jax
import jax.numpy as jnp
from jax import lax
from jax.experimental import pallas as pl
from jax.experimental.pallas import tpu as pltpu
from jax.sharding import PartitionSpec as P

ROPE_BASE = 1000000.0
HD = 128
NEG = -1e30
MESH = pl.DeviceIdType.MESH
NT = (((1,), (1,)), ((), ()))
LATE = 6
STAGES = ((0, 4, 2), (4, 4, 2))


def kernel(
    NY, NX, NTEN, PIECE, STEPS,
    rows_hbm, hidden_hbm, cache_hbm, query_hbm, bias_hbm, len_hbm,
    cols, att,
    parts, hidden, cache, query, bias_ref, len_ref, mine, other,
    part_send, part_recv, send, one_y, one_x, all_y, all_x, hand, heard, load, pair_send, pair_recv,
):
    rep = lax.axis_index("replica")
    ten = lax.axis_index("tensor")
    core = lax.rem(rep, 2)
    chip = lax.div(rep, 2)
    x = lax.rem(chip, NX)
    y = lax.div(chip, NX)
    parity = lax.rem(ten, 2)
    block = NTEN * PIECE

    def replica(dy, dx, c=None):
        yy = lax.rem(y + dy + 2 * NY, NY)
        xx = lax.rem(x + dx + 2 * NX, NX)
        return (yy * NX + xx) * 2 + (core if c is None else c)

    def wrap(i, n):
        return lax.rem(i + 2 * n, n)

    sibling = replica(0, 0, 1 - core)
    near = sorted(range(1 - NX // 2, NX // 2 + 1), key=abs)[1:]
    ahead = sorted(range(1 - NY // 2, NY // 2 + 1), key=abs)[1:]
    layer = lax.div(ten, 2)
    partner = ten + 1 - 2 * parity

    barrier = pltpu.get_barrier_semaphore()
    late = layer >= LATE
    plane = [replica(0, d) for d in near] + [replica(d, 0) for d in ahead] + [sibling]

    @pl.when(jnp.logical_not(late))
    def _():
        for r in plane:
            pl.semaphore_signal(barrier, inc=1, device_id=(r, ten), device_id_type=MESH)
        pl.semaphore_signal(barrier, inc=1, device_id=(rep, partner), device_id_type=MESH)

    for p in reversed(range(2, NTEN)):

        @pl.when(p >= 2 * layer + 2)
        def _():
            pl.semaphore_signal(barrier, inc=1, device_id=(rep, p), device_id_type=MESH)

    loads = [
        pltpu.make_async_copy(query_hbm, query, load.at[0]),
        pltpu.make_async_copy(cache_hbm, cache, load.at[1]),
        pltpu.make_async_copy(hidden_hbm, hidden, load.at[2]),
        pltpu.make_async_copy(
            rows_hbm.at[:, pl.ds(pl.multiple_of(ten * HD, HD), HD)], parts.at[ten], load.at[3]
        ),
        pltpu.make_async_copy(len_hbm, len_ref, load.at[4]),
        pltpu.make_async_copy(bias_hbm, bias_ref, load.at[5]),
    ]
    for i in (3, 4, 5, 0, 1, 2):
        loads[i].start()
    @pl.when(late)
    def _():
        pl.semaphore_wait(barrier, 2 * layer)

    @pl.when(jnp.logical_not(late))
    def _():
        pl.semaphore_wait(barrier, len(plane) + 2 * layer + 1)

    def give(p):
        pltpu.make_async_remote_copy(
            src_ref=rows_hbm.at[:, pl.ds(pl.multiple_of(p * HD, HD), HD)], dst_ref=parts.at[ten],
            send_sem=part_send, recv_sem=part_recv.at[ten],
            device_id=(rep, p), device_id_type=MESH,
        ).start()

    def take(p):
        pltpu.make_async_copy(parts.at[p], parts.at[p], part_recv.at[p]).wait()

    for p in range(NTEN - 2):

        @pl.when(p < 2 * layer)
        def _():
            give(p)

    @pl.when(jnp.logical_not(late))
    def _():
        give(partner)

    unit = 2 * PIECE

    def along_y(yy_or_all, xx, stage, c):
        first, _, part = STAGES[stage]
        return cols.at[yy_or_all, xx, c, pl.ds(first * unit, part * unit), :]

    def along_x(yy, xx_or_all, stage, c):
        first, n, part = STAGES[stage]
        return cols.at[yy, xx_or_all, c, pl.ds((first + part) * unit, (n - part) * unit), :]

    def push(ref, to, kind, recv_sem):
        pltpu.make_async_remote_copy(
            src_ref=ref, dst_ref=ref, send_sem=send.at[kind], recv_sem=recv_sem,
            device_id=(to, ten), device_id_type=MESH,
        ).start()

    def arrived(ref, recv_sem):
        pltpu.make_async_copy(ref, ref, recv_sem).wait()

    every = slice(None)

    def begin(stage):
        first, n, _ = STAGES[stage]
        pieces = [parts[p].astype(jnp.float32) for p in range(2 * first, 2 * (first + n))]
        cols[y, x, core, pl.ds(first * unit, n * unit), :] = jnp.concatenate(
            pieces, axis=0
        ).astype(jnp.bfloat16)
        for d in reversed(ahead):
            push(along_y(y, x, stage, core), replica(d, 0), 0, one_y.at[stage, y])
        for d in reversed(near):
            push(along_x(y, x, stage, core), replica(0, d), 0, one_x.at[stage, x])

    def turn(stage):
        for d in ahead:
            yy = wrap(y - d, NY)
            arrived(along_y(yy, x, stage, core), one_y.at[stage, yy])
        for d in reversed(near):
            push(along_y(every, x, stage, core), replica(0, d), 1, all_x.at[stage, x])
        for d in near:
            xx = wrap(x - d, NX)
            arrived(along_x(y, xx, stage, core), one_x.at[stage, xx])
        for d in reversed(ahead):
            push(along_x(y, every, stage, core), replica(d, 0), 2, all_y.at[stage, y])

    def finish(stage):
        for d in ahead:
            yy = wrap(y - d, NY)
            arrived(along_x(yy, every, stage, core), all_y.at[stage, yy])
        push(along_x(every, every, stage, core), sibling, 3, hand.at[stage, 1])
        for d in near:
            xx = wrap(x - d, NX)
            arrived(along_y(every, xx, stage, core), all_x.at[stage, xx])
        push(along_y(every, every, stage, core), sibling, 3, hand.at[stage, 0])

    def got(stage):
        arrived(along_x(every, every, stage, 1 - core), hand.at[stage, 1])
        arrived(along_y(every, every, stage, 1 - core), hand.at[stage, 0])

    lane = lax.broadcasted_iota(jnp.int32, (1, HD), 1)
    half = lax.rem(lane, HD // 2).astype(jnp.float32)
    frequency = jnp.exp(half * (-2.0 * math.log(ROPE_BASE) / HD))
    step = lax.broadcasted_iota(jnp.int32, (STEPS, HD), 0)
    n_rows = hidden.shape[0] // STEPS
    loads[4].wait()
    position = jnp.concatenate([step + len_ref[b] for b in range(n_rows)], axis=0)
    angle = position.astype(jnp.float32) * frequency
    cosine = jnp.cos(angle)
    sine = jnp.sin(angle) * jnp.where(lane < HD // 2, -1.0, 1.0)

    scale = 1.0 / math.sqrt(HD)
    n_att = query.shape[0]
    groups = query.shape[2] // HD
    queries, peaks, totals, sums = [], [], [], []

    def attend_cached(i):
        if i == 0:
            loads[0].wait()
            loads[1].wait()
        wide = query[i].astype(jnp.float32)
        q = jnp.concatenate([wide[:, g * HD : (g + 1) * HD] for g in range(groups)], axis=0)
        q = q.astype(jnp.bfloat16)
        s = lax.dot_general(q, cache[i, :, :HD], NT, preferred_element_type=jnp.float32) * scale
        place = lax.broadcasted_iota(jnp.int32, s.shape, 1)
        s = jnp.where(place < len_ref[parity * n_att + i], s, NEG)
        m = jnp.max(s, axis=1, keepdims=True)
        e = jnp.exp(s - m)
        queries.append(q)
        peaks.append(m)
        totals.append(jnp.sum(e, axis=1, keepdims=True))
        sums.append(
            jnp.dot(e.astype(jnp.bfloat16), cache[i, :, HD:], preferred_element_type=jnp.float32)
        )


    def project(yy):
        wide = NX * 2 * block
        return jnp.dot(
            hidden[:, yy * wide : (yy + 1) * wide], cols[yy].reshape(wide, HD), preferred_element_type=jnp.float32
        )

    for i in range(n_att):
        attend_cached(i)
    loads[2].wait()

    def answer(first, end):
        for p in range(2 * first, 2 * end, 2):

            @pl.when(p > 2 * layer)
            def _():
                take(p)
                take(p + 1)
                give(p)
                give(p + 1)

    def meet(first, end):
        for p in range(2 * first, 2 * end, 2):

            @pl.when(p < 2 * layer)
            def _():
                take(p)
                take(p + 1)

            if p == 0:

                @pl.when(late)
                def _():
                    give(partner)

            @pl.when(p == 2 * layer)
            def _():
                take(partner)

    def hear(first):
        for p in range(2 * first, NTEN, 2):

            @pl.when(layer == 0)
            def _():
                take(p)
                take(p + 1)
                for r in plane:
                    pl.semaphore_signal(
                        heard.at[p // 2 - first], inc=1, device_id=(r, ten), device_id_type=MESH
                    )

            @pl.when(layer > 0)
            def _():
                take(p)
                take(p + 1)
                give(p)
                give(p + 1)

    def confirm(first):
        for p in range(2 * first, NTEN, 2):

            @pl.when(layer == 0)
            def _():
                pl.semaphore_wait(heard.at[p // 2 - first], len(plane))
                give(p)
                give(p + 1)

    loads[3].wait()

    @pl.when(layer < 3)
    def _():
        answer(0, 4)
        meet(0, 4)
        begin(0)
        answer(4, LATE)
        hear(LATE)
        begin(1)
        turn(0)
        confirm(LATE)
        turn(1)

    @pl.when(layer >= 3)
    def _():
        answer(3, 8)
        meet(0, 4)
        begin(0)
        meet(4, 8)
        begin(1)
        turn(0)
        turn(1)

    finish(0)
    got(0)
    finish(1)
    got(1)
    projected = project(0)
    for yy in range(1, NY):
        projected += project(yy)

    loads[5].wait()
    whole = projected + bias_ref[...].astype(jnp.float32)
    rotated = whole * cosine + pltpu.roll(whole, HD // 2, 1) * sine
    whole = jnp.where(parity == 0, rotated, whole).astype(jnp.bfloat16)
    n_half = whole.shape[0] // 2
    mine[0] = whole[:n_half]
    mine[1] = whole[n_half:]
    exchange = pltpu.make_async_remote_copy(
        src_ref=mine.at[1 - parity], dst_ref=other, send_sem=pair_send, recv_sem=pair_recv,
        device_id=(rep, partner), device_id_type=MESH,
    )
    exchange.start()
    exchange.wait()
    kept, got = mine[parity], other[...]
    new_keys = jnp.where(parity == 0, kept, got)
    new_values = jnp.where(parity == 0, got, kept)

    q = jnp.concatenate(queries, axis=0)
    s = lax.dot_general(q, new_keys, NT, preferred_element_type=jnp.float32) * scale
    of_query = lax.broadcasted_iota(jnp.int32, s.shape, 0)
    of_key = lax.broadcasted_iota(jnp.int32, s.shape, 1)
    same_row = lax.div(of_query, groups * STEPS) == lax.div(of_key, STEPS)
    causal = lax.rem(of_key, STEPS) <= lax.rem(of_query, STEPS)
    s = jnp.where(same_row & causal, s, NEG)
    old_peak = jnp.concatenate(peaks, axis=0)
    peak = jnp.maximum(old_peak, jnp.max(s, axis=1, keepdims=True))
    e = jnp.exp(s - peak)
    shrink = jnp.exp(old_peak - peak)
    total = jnp.concatenate(totals, axis=0) * shrink + jnp.sum(e, axis=1, keepdims=True)
    out = jnp.concatenate(sums, axis=0) * shrink
    out += jnp.dot(e.astype(jnp.bfloat16), new_values, preferred_element_type=jnp.float32)
    out = out / total
    for i in range(n_att):
        base = i * groups * STEPS
        att[i] = jnp.concatenate(
            [out[base + g * STEPS : base + (g + 1) * STEPS] for g in range(groups)], axis=1
        ).astype(jnp.bfloat16)

    given = parts.at[pl.ds(0, NTEN - 1)]
    pltpu.make_async_copy(given, given, part_send).wait()
    for kind, ref in enumerate(
        (
            cols.at[0, pl.ds(0, (NX + NY - 2) // 2), 0],
            cols.at[pl.ds(0, NY // 2), pl.ds(0, NX - 1), 0],
            cols.at[pl.ds(0, NY - 1), pl.ds(0, NX // 2), 0],
            cols.at[pl.ds(0, NY // 2)],
        )
    ):
        pltpu.make_async_copy(ref, ref, send.at[kind]).wait()


def solution(mesh):
    n_rep, n_ten = mesh.shape["replica"], mesh.shape["tensor"]
    NX = 8
    NY = n_rep // (2 * NX)

    def per_device(hidden_rows, prior_bias, cache_blocks, queries, cache_lengths, updated_rows):
        n_rows, steps, width = hidden_rows.shape
        piece = updated_rows.shape[0]
        vmem = pl.BlockSpec(memory_space=pltpu.VMEM)
        block = n_ten * piece
        attended, columns = pl.pallas_call(
            functools.partial(kernel, NY, NX, n_ten, piece, steps),
            out_shape=(
                jax.ShapeDtypeStruct((NY, NX, 2, block, HD), jnp.bfloat16),
                jax.ShapeDtypeStruct(queries.shape[1:], jnp.bfloat16),
            ),
            in_specs=[pl.BlockSpec(memory_space=pltpu.HBM)] * 6,
            out_specs=(vmem, vmem),
            scratch_shapes=[
                pltpu.VMEM((n_ten, piece, HD), jnp.bfloat16),
                pltpu.VMEM((n_rows * steps, width), jnp.bfloat16),
                pltpu.VMEM(cache_blocks.shape[1:], jnp.bfloat16),
                pltpu.VMEM(queries.shape[1:], jnp.bfloat16),
                pltpu.VMEM((1, HD), jnp.bfloat16),
                pltpu.SMEM((n_rows,), jnp.int32),
                pltpu.VMEM((2, n_rows * steps // 2, HD), jnp.bfloat16),
                pltpu.VMEM((n_rows * steps // 2, HD), jnp.bfloat16),
                pltpu.SemaphoreType.DMA,
                pltpu.SemaphoreType.DMA((n_ten,)),
                pltpu.SemaphoreType.DMA((4,)),
                *[pltpu.SemaphoreType.DMA((len(STAGES), n)) for n in (NY, NX, NY, NX, 2)],
                pltpu.SemaphoreType.REGULAR((n_ten // 2 - LATE,)),
                pltpu.SemaphoreType.DMA((6,)),
                pltpu.SemaphoreType.DMA,
                pltpu.SemaphoreType.DMA,
            ],
            compiler_params=pltpu.CompilerParams(
                collective_id=0, has_side_effects=True, vmem_limit_bytes=40 << 20
            ),
        )(
            *(
                pltpu.with_memory_space_constraint(a, pltpu.HBM)
                for a in (
                    updated_rows,
                    hidden_rows.reshape(n_rows * steps, width),
                    cache_blocks[0],
                    queries[0],
                    prior_bias.reshape(1, HD),
                    cache_lengths,
                )
            )
        )[::-1]
        return attended[None], columns.reshape(n_rep * block, HD)

    return jax.shard_map(
        per_device,
        mesh=mesh,
        in_specs=(
            P("replica", None, None),
            P("tensor"),
            P("tensor", "replica", None, None),
            P("tensor", "replica", None, None),
            P("replica"),
            P(("replica", "tensor"), None),
        ),
        out_specs=(P("tensor", "replica", None, None), P(None, "tensor")),
        check_vma=False,
    )
```

```python
import functools
import math

import jax
import jax.numpy as jnp
from jax import lax
from jax.experimental import pallas as pl
from jax.experimental.pallas import tpu as pltpu
from jax.sharding import PartitionSpec as P

ROPE_BASE = 1000000.0
HD = 128
NEG = -1e30
MESH = pl.DeviceIdType.MESH
NT = (((1,), (1,)), ((), ()))
LATE = 6
STAGES = ((0, 3, 2), (3, 1, 0), (4, 4, 2), (0, 4, 2), (4, 4, 2))


def kernel(
    NY, NX, NTEN, PIECE, STEPS,
    rows_hbm, hidden_hbm, cache_hbm, query_hbm, bias_hbm, len_hbm,
    cols, q_out, peak_out, total_out, sum_out, keys, values,
    parts, hidden, cache, query, bias_ref, len_ref, mine, other,
    part_send, part_recv, send, one_y, one_x, all_y, all_x, hand, heard, load, pair_send, pair_recv,
):
    rep = lax.axis_index("replica")
    ten = lax.axis_index("tensor")
    core = lax.rem(rep, 2)
    chip = lax.div(rep, 2)
    x = lax.rem(chip, NX)
    y = lax.div(chip, NX)
    parity = lax.rem(ten, 2)
    block = NTEN * PIECE

    def replica(dy, dx, c=None):
        yy = lax.rem(y + dy + 2 * NY, NY)
        xx = lax.rem(x + dx + 2 * NX, NX)
        return (yy * NX + xx) * 2 + (core if c is None else c)

    def wrap(i, n):
        return lax.rem(i + 2 * n, n)

    sibling = replica(0, 0, 1 - core)
    near = sorted(range(1 - NX // 2, NX // 2 + 1), key=abs)[1:]
    ahead = sorted(range(1 - NY // 2, NY // 2 + 1), key=abs)[1:]
    layer = lax.div(ten, 2)
    partner = ten + 1 - 2 * parity

    barrier = pltpu.get_barrier_semaphore()
    late = layer >= LATE
    plane = [replica(0, d) for d in near] + [replica(d, 0) for d in ahead] + [sibling]

    @pl.when(jnp.logical_not(late))
    def _():
        for r in plane:
            pl.semaphore_signal(barrier, inc=1, device_id=(r, ten), device_id_type=MESH)
        pl.semaphore_signal(barrier, inc=1, device_id=(rep, partner), device_id_type=MESH)

    for p in reversed(range(2, NTEN)):

        @pl.when(p >= 2 * layer + 2)
        def _():
            pl.semaphore_signal(barrier, inc=1, device_id=(rep, p), device_id_type=MESH)

    loads = [
        pltpu.make_async_copy(query_hbm, query, load.at[0]),
        pltpu.make_async_copy(cache_hbm, cache, load.at[1]),
        pltpu.make_async_copy(hidden_hbm, hidden, load.at[2]),
        pltpu.make_async_copy(
            rows_hbm.at[:, pl.ds(pl.multiple_of(ten * HD, HD), HD)], parts.at[ten], load.at[3]
        ),
        pltpu.make_async_copy(len_hbm, len_ref, load.at[4]),
        pltpu.make_async_copy(bias_hbm, bias_ref, load.at[5]),
    ]
    for i in (3, 4, 5, 0, 1, 2):
        loads[i].start()
    @pl.when(late)
    def _():
        pl.semaphore_wait(barrier, 2 * layer)

    @pl.when(jnp.logical_not(late))
    def _():
        pl.semaphore_wait(barrier, len(plane) + 2 * layer + 1)

    def give(p):
        pltpu.make_async_remote_copy(
            src_ref=rows_hbm.at[:, pl.ds(pl.multiple_of(p * HD, HD), HD)], dst_ref=parts.at[ten],
            send_sem=part_send, recv_sem=part_recv.at[ten],
            device_id=(rep, p), device_id_type=MESH,
        ).start()

    def take(p):
        pltpu.make_async_copy(parts.at[p], parts.at[p], part_recv.at[p]).wait()

    for p in range(NTEN - 2):

        @pl.when(p < 2 * layer)
        def _():
            give(p)

    @pl.when(jnp.logical_not(late))
    def _():
        give(partner)

    unit = 2 * PIECE

    def along_y(yy_or_all, xx, stage, c):
        first, _, part = STAGES[stage]
        return cols.at[yy_or_all, xx, c, pl.ds(first * unit, part * unit), :]

    def along_x(yy, xx_or_all, stage, c):
        first, n, part = STAGES[stage]
        return cols.at[yy, xx_or_all, c, pl.ds((first + part) * unit, (n - part) * unit), :]

    def push(ref, to, kind, recv_sem):
        pltpu.make_async_remote_copy(
            src_ref=ref, dst_ref=ref, send_sem=send.at[kind], recv_sem=recv_sem,
            device_id=(to, ten), device_id_type=MESH,
        ).start()

    def arrived(ref, recv_sem):
        pltpu.make_async_copy(ref, ref, recv_sem).wait()

    every = slice(None)

    def begin(stage):
        first, n, part = STAGES[stage]
        pieces = [parts[p].astype(jnp.float32) for p in range(2 * first, 2 * (first + n))]
        cols[y, x, core, pl.ds(first * unit, n * unit), :] = jnp.concatenate(
            pieces, axis=0
        ).astype(jnp.bfloat16)
        if part:
            for d in reversed(ahead):
                push(along_y(y, x, stage, core), replica(d, 0), 0, one_y.at[stage, y])
        for d in reversed(near):
            push(along_x(y, x, stage, core), replica(0, d), 0, one_x.at[stage, x])

    def turn(stage):
        if STAGES[stage][2]:
            for d in ahead:
                yy = wrap(y - d, NY)
                arrived(along_y(yy, x, stage, core), one_y.at[stage, yy])
            for d in reversed(near):
                push(along_y(every, x, stage, core), replica(0, d), 1, all_x.at[stage, x])
        for d in near:
            xx = wrap(x - d, NX)
            arrived(along_x(y, xx, stage, core), one_x.at[stage, xx])
        for d in reversed(ahead):
            push(along_x(y, every, stage, core), replica(d, 0), 2, all_y.at[stage, y])

    def finish(stage):
        for d in ahead:
            yy = wrap(y - d, NY)
            arrived(along_x(yy, every, stage, core), all_y.at[stage, yy])
        push(along_x(every, every, stage, core), sibling, 3, hand.at[stage, 1])
        if STAGES[stage][2]:
            for d in near:
                xx = wrap(x - d, NX)
                arrived(along_y(every, xx, stage, core), all_x.at[stage, xx])
            push(along_y(every, every, stage, core), sibling, 3, hand.at[stage, 0])

    def got(stage):
        arrived(along_x(every, every, stage, 1 - core), hand.at[stage, 1])
        if STAGES[stage][2]:
            arrived(along_y(every, every, stage, 1 - core), hand.at[stage, 0])

    lane = lax.broadcasted_iota(jnp.int32, (1, HD), 1)
    half = lax.rem(lane, HD // 2).astype(jnp.float32)
    frequency = jnp.exp(half * (-2.0 * math.log(ROPE_BASE) / HD))
    step = lax.broadcasted_iota(jnp.int32, (STEPS, HD), 0)
    n_rows = hidden.shape[0] // STEPS
    loads[4].wait()
    position = jnp.concatenate([step + len_ref[b] for b in range(n_rows)], axis=0)
    angle = position.astype(jnp.float32) * frequency
    cosine = jnp.cos(angle)
    sine = jnp.sin(angle) * jnp.where(lane < HD // 2, -1.0, 1.0)

    scale = 1.0 / math.sqrt(HD)
    n_att = query.shape[0]
    groups = query.shape[2] // HD

    def attend_cached(i):
        if i == 0:
            loads[0].wait()
            loads[1].wait()
        wide = query[i].astype(jnp.float32)
        q = jnp.concatenate([wide[:, g * HD : (g + 1) * HD] for g in range(groups)], axis=0)
        q = q.astype(jnp.bfloat16)
        s = lax.dot_general(q, cache[i, :, :HD], NT, preferred_element_type=jnp.float32) * scale
        place = lax.broadcasted_iota(jnp.int32, s.shape, 1)
        s = jnp.where(place < len_ref[parity * n_att + i], s, NEG)
        m = jnp.max(s, axis=1, keepdims=True)
        e = jnp.exp(s - m)
        here = pl.ds(i * groups * STEPS, groups * STEPS)
        q_out[here, :] = q
        peak_out[here, :] = jnp.broadcast_to(m, q.shape)
        total_out[here, :] = jnp.broadcast_to(jnp.sum(e, axis=1, keepdims=True), q.shape)
        sum_out[here, :] = jnp.dot(
            e.astype(jnp.bfloat16), cache[i, :, HD:], preferred_element_type=jnp.float32
        )

    def project(yy):
        wide = NX * 2 * block
        return jnp.dot(
            hidden[:, yy * wide : (yy + 1) * wide], cols[yy].reshape(wide, HD), preferred_element_type=jnp.float32
        )

    for i in range(n_att):
        attend_cached(i)
    loads[2].wait()

    def answer(first, end):
        for p in range(2 * first, 2 * end, 2):

            @pl.when(p > 2 * layer)
            def _():
                take(p)
                take(p + 1)
                give(p)
                give(p + 1)

    def meet(first, end):
        for p in range(2 * first, 2 * end, 2):

            @pl.when(p < 2 * layer)
            def _():
                take(p)
                take(p + 1)

            if p == 0:

                @pl.when(late)
                def _():
                    give(partner)

            @pl.when(p == 2 * layer)
            def _():
                take(partner)

    def hear():
        for p in range(2 * LATE, NTEN):
            take(p)

    def tell():
        for l in range(LATE, NTEN // 2):
            for r in plane:
                pl.semaphore_signal(
                    heard.at[l - LATE], inc=1, device_id=(r, ten), device_id_type=MESH
                )

    def confirm():
        for l in range(LATE, NTEN // 2):
            pl.semaphore_wait(heard.at[l - LATE], len(plane))
            give(2 * l)
            give(2 * l + 1)

    loads[3].wait()

    @pl.when(layer == 0)
    def _():
        answer(0, 3)
        meet(0, 3)
        begin(0)
        answer(3, 4)
        begin(1)
        turn(0)
        answer(4, LATE)
        hear()
        begin(2)
        tell()
        turn(1)
        turn(2)
        confirm()
        finish(0)
        finish(1)
        got(0)
        got(1)
        finish(2)
        got(2)

    @pl.when((layer > 0) & (layer < 3))
    def _():
        answer(0, 4)
        meet(0, 4)
        begin(3)
        answer(4, 8)
        begin(4)
        turn(3)
        turn(4)
        finish(3)
        got(3)
        finish(4)
        got(4)

    @pl.when(layer >= 3)
    def _():
        answer(3, 8)
        meet(0, 4)
        begin(3)
        meet(4, 8)
        begin(4)
        turn(3)
        turn(4)
        finish(3)
        got(3)
        finish(4)
        got(4)

    projected = project(0)
    for yy in range(1, NY):
        projected += project(yy)

    loads[5].wait()
    whole = projected + bias_ref[...].astype(jnp.float32)
    rotated = whole * cosine + pltpu.roll(whole, HD // 2, 1) * sine
    whole = jnp.where(parity == 0, rotated, whole).astype(jnp.bfloat16)
    n_half = whole.shape[0] // 2
    mine[0] = whole[:n_half]
    mine[1] = whole[n_half:]
    exchange = pltpu.make_async_remote_copy(
        src_ref=mine.at[1 - parity], dst_ref=other, send_sem=pair_send, recv_sem=pair_recv,
        device_id=(rep, partner), device_id_type=MESH,
    )
    exchange.start()
    exchange.wait()
    kept, theirs = mine[parity], other[...]
    new_keys = jnp.where(parity == 0, kept, theirs)
    new_values = jnp.where(parity == 0, theirs, kept)

    keys[...] = new_keys
    values[...] = new_values

    given = parts.at[pl.ds(0, NTEN - 1)]
    pltpu.make_async_copy(given, given, part_send).wait()
    for kind, ref in enumerate(
        (
            cols.at[0, pl.ds(0, (NX + NY - 2) // 2), 0],
            cols.at[pl.ds(0, NY // 2), pl.ds(0, NX - 1), 0],
            cols.at[pl.ds(0, NY - 1), pl.ds(0, NX // 2), 0],
            cols.at[pl.ds(0, NY // 2)],
        )
    ):
        pltpu.make_async_copy(ref, ref, send.at[kind]).wait()


def join(
    STEPS,
    cols, q_ref, peak_ref, total_ref, sum_ref, keys, values,
    cols_out, att_out,
    att, sems,
):
    out = pltpu.make_async_copy(cols, cols_out, sems.at[0])
    out.start()
    scale = 1.0 / math.sqrt(HD)
    n_att, _, wide = att.shape
    groups = wide // HD
    s = lax.dot_general(q_ref[...], keys[...], NT, preferred_element_type=jnp.float32) * scale
    of_query = lax.broadcasted_iota(jnp.int32, s.shape, 0)
    of_key = lax.broadcasted_iota(jnp.int32, s.shape, 1)
    same_row = lax.div(of_query, groups * STEPS) == lax.div(of_key, STEPS)
    causal = lax.rem(of_key, STEPS) <= lax.rem(of_query, STEPS)
    s = jnp.where(same_row & causal, s, NEG)
    old_peak = peak_ref[...]
    peak = jnp.maximum(old_peak, jnp.max(s, axis=1, keepdims=True))
    e = jnp.exp(s - peak[:, : s.shape[1]])
    shrink = jnp.exp(old_peak - peak)
    total = total_ref[...] * shrink + jnp.sum(e, axis=1, keepdims=True)
    mixed = sum_ref[...] * shrink
    mixed += jnp.dot(e.astype(jnp.bfloat16), values[...], preferred_element_type=jnp.float32)
    mixed = mixed / total
    for i in range(n_att):
        base = i * groups * STEPS
        att[i] = jnp.concatenate(
            [mixed[base + g * STEPS : base + (g + 1) * STEPS] for g in range(groups)], axis=1
        ).astype(jnp.bfloat16)
    done = pltpu.make_async_copy(att, att_out, sems.at[1])
    done.start()
    done.wait()
    out.wait()


def solution(mesh):
    n_rep, n_ten = mesh.shape["replica"], mesh.shape["tensor"]
    NX = 8
    NY = n_rep // (2 * NX)

    def per_device(hidden_rows, prior_bias, cache_blocks, queries, cache_lengths, updated_rows):
        n_rows, steps, width = hidden_rows.shape
        piece = updated_rows.shape[0]
        vmem = pl.BlockSpec(memory_space=pltpu.VMEM)
        block = n_ten * piece
        n_att, _, q_width = queries.shape[1:]
        n_query = n_att * steps * (q_width // HD)
        half = n_rows * steps // 2
        gathered = pl.pallas_call(
            functools.partial(kernel, NY, NX, n_ten, piece, steps),
            out_shape=(
                jax.ShapeDtypeStruct((NY, NX, 2, block, HD), jnp.bfloat16),
                jax.ShapeDtypeStruct((n_query, HD), jnp.bfloat16),
                *[jax.ShapeDtypeStruct((n_query, HD), jnp.float32)] * 3,
                *[jax.ShapeDtypeStruct((half, HD), jnp.bfloat16)] * 2,
            ),
            in_specs=[pl.BlockSpec(memory_space=pltpu.HBM)] * 6,
            out_specs=(vmem,) * 7,
            scratch_shapes=[
                pltpu.VMEM((n_ten, piece, HD), jnp.bfloat16),
                pltpu.VMEM((n_rows * steps, width), jnp.bfloat16),
                pltpu.VMEM(cache_blocks.shape[1:], jnp.bfloat16),
                pltpu.VMEM(queries.shape[1:], jnp.bfloat16),
                pltpu.VMEM((1, HD), jnp.bfloat16),
                pltpu.SMEM((n_rows,), jnp.int32),
                pltpu.VMEM((2, n_rows * steps // 2, HD), jnp.bfloat16),
                pltpu.VMEM((n_rows * steps // 2, HD), jnp.bfloat16),
                pltpu.SemaphoreType.DMA,
                pltpu.SemaphoreType.DMA((n_ten,)),
                pltpu.SemaphoreType.DMA((4,)),
                *[pltpu.SemaphoreType.DMA((len(STAGES), n)) for n in (NY, NX, NY, NX, 2)],
                pltpu.SemaphoreType.REGULAR((n_ten // 2 - LATE,)),
                pltpu.SemaphoreType.DMA((6,)),
                pltpu.SemaphoreType.DMA,
                pltpu.SemaphoreType.DMA,
            ],
            compiler_params=pltpu.CompilerParams(
                collective_id=0, has_side_effects=True, vmem_limit_bytes=40 << 20
            ),
        )(
            *(
                pltpu.with_memory_space_constraint(a, pltpu.HBM)
                for a in (
                    updated_rows,
                    hidden_rows.reshape(n_rows * steps, width),
                    cache_blocks[0],
                    queries[0],
                    prior_bias.reshape(1, HD),
                    cache_lengths,
                )
            )
        )
        columns, attended = pl.pallas_call(
            functools.partial(join, steps),
            out_shape=(
                jax.ShapeDtypeStruct(gathered[0].shape, jnp.bfloat16),
                jax.ShapeDtypeStruct(queries.shape[1:], jnp.bfloat16),
            ),
            in_specs=[pl.BlockSpec(memory_space=pl.ANY)] + [vmem] * 6,
            out_specs=(pl.BlockSpec(memory_space=pltpu.HBM),) * 2,
            scratch_shapes=[
                pltpu.VMEM(queries.shape[1:], jnp.bfloat16),
                pltpu.SemaphoreType.DMA((2,)),
            ],
            compiler_params=pltpu.CompilerParams(vmem_limit_bytes=16 << 20),
        )(*gathered)
        return attended[None], columns.reshape(n_rep * block, HD)

    return jax.shard_map(
        per_device,
        mesh=mesh,
        in_specs=(
            P("replica", None, None),
            P("tensor"),
            P("tensor", "replica", None, None),
            P("tensor", "replica", None, None),
            P("replica"),
            P(("replica", "tensor"), None),
        ),
        out_specs=(P("tensor", "replica", None, None), P(None, "tensor")),
        check_vma=False,
    )
```

```python
import functools
import math

import jax
import jax.numpy as jnp
from jax import lax
from jax.experimental import pallas as pl
from jax.experimental.pallas import tpu as pltpu
from jax.sharding import PartitionSpec as P

ROPE_BASE = 1000000.0
HD = 128
NEG = -1e30
MESH = pl.DeviceIdType.MESH
NT = (((1,), (1,)), ((), ()))
LATE = 6
STAGES = ((0, 3, 2), (3, 1, 0), (4, 4, 2), (0, 4, 2), (4, 4, 2))


def kernel(
    NY, NX, NTEN, PIECE, STEPS,
    rows_hbm, hidden_hbm, cache_hbm, query_hbm, bias_hbm, len_hbm,
    cols, q_out, peak_out, total_out, sum_out, keys, values,
    parts, hidden, cache, query, bias_ref, len_ref, mine, other,
    part_send, part_recv, send, one_y, one_x, all_y, all_x, hand, heard, load, pair_send, pair_recv,
):
    rep = lax.axis_index("replica")
    ten = lax.axis_index("tensor")
    core = lax.rem(rep, 2)
    chip = lax.div(rep, 2)
    x = lax.rem(chip, NX)
    y = lax.div(chip, NX)
    parity = lax.rem(ten, 2)
    block = NTEN * PIECE

    def replica(dy, dx, c=None):
        yy = lax.rem(y + dy + 2 * NY, NY)
        xx = lax.rem(x + dx + 2 * NX, NX)
        return (yy * NX + xx) * 2 + (core if c is None else c)

    def wrap(i, n):
        return lax.rem(i + 2 * n, n)

    sibling = replica(0, 0, 1 - core)
    near = sorted(range(1 - NX // 2, NX // 2 + 1), key=abs)[1:]
    ahead = sorted(range(1 - NY // 2, NY // 2 + 1), key=abs)[1:]
    layer = lax.div(ten, 2)
    partner = ten + 1 - 2 * parity

    barrier = pltpu.get_barrier_semaphore()
    late = layer >= LATE
    plane = [replica(0, d) for d in near] + [replica(d, 0) for d in ahead] + [sibling]

    @pl.when(jnp.logical_not(late))
    def _():
        for r in plane:
            pl.semaphore_signal(barrier, inc=1, device_id=(r, ten), device_id_type=MESH)
        pl.semaphore_signal(barrier, inc=1, device_id=(rep, partner), device_id_type=MESH)

    for p in reversed(range(2, NTEN)):

        @pl.when(p >= 2 * layer + 2)
        def _():
            pl.semaphore_signal(barrier, inc=1, device_id=(rep, p), device_id_type=MESH)

    loads = [
        pltpu.make_async_copy(query_hbm, query, load.at[0]),
        pltpu.make_async_copy(cache_hbm, cache, load.at[1]),
        pltpu.make_async_copy(hidden_hbm, hidden, load.at[2]),
        pltpu.make_async_copy(
            rows_hbm.at[:, pl.ds(pl.multiple_of(ten * HD, HD), HD)], parts.at[ten], load.at[3]
        ),
        pltpu.make_async_copy(len_hbm, len_ref, load.at[4]),
        pltpu.make_async_copy(bias_hbm, bias_ref, load.at[5]),
    ]
    for i in (3, 4, 5, 0, 1, 2):
        loads[i].start()
    @pl.when(late)
    def _():
        pl.semaphore_wait(barrier, 2 * layer)

    @pl.when(jnp.logical_not(late))
    def _():
        pl.semaphore_wait(barrier, len(plane) + 2 * layer + 1)

    def give(p):
        pltpu.make_async_remote_copy(
            src_ref=rows_hbm.at[:, pl.ds(pl.multiple_of(p * HD, HD), HD)], dst_ref=parts.at[ten],
            send_sem=part_send, recv_sem=part_recv.at[ten],
            device_id=(rep, p), device_id_type=MESH,
        ).start()

    def take(p):
        pltpu.make_async_copy(parts.at[p], parts.at[p], part_recv.at[p]).wait()

    for p in range(NTEN - 2):

        @pl.when(p < 2 * layer)
        def _():
            give(p)

    @pl.when(jnp.logical_not(late))
    def _():
        give(partner)

    unit = 2 * PIECE

    def along_y(yy_or_all, xx, stage, c):
        first, _, part = STAGES[stage]
        return cols.at[yy_or_all, xx, c, pl.ds(first * unit, part * unit), :]

    def along_x(yy, xx_or_all, stage, c):
        first, n, part = STAGES[stage]
        return cols.at[yy, xx_or_all, c, pl.ds((first + part) * unit, (n - part) * unit), :]

    def push(ref, to, kind, recv_sem):
        pltpu.make_async_remote_copy(
            src_ref=ref, dst_ref=ref, send_sem=send.at[kind], recv_sem=recv_sem,
            device_id=(to, ten), device_id_type=MESH,
        ).start()

    def arrived(ref, recv_sem):
        pltpu.make_async_copy(ref, ref, recv_sem).wait()

    every = slice(None)

    def begin(stage):
        first, n, part = STAGES[stage]
        pieces = [parts[p].astype(jnp.float32) for p in range(2 * first, 2 * (first + n))]
        cols[y, x, core, pl.ds(first * unit, n * unit), :] = jnp.concatenate(
            pieces, axis=0
        ).astype(jnp.bfloat16)
        if part:
            for d in reversed(ahead):
                push(along_y(y, x, stage, core), replica(d, 0), 0, one_y.at[stage, y])
        for d in reversed(near):
            push(along_x(y, x, stage, core), replica(0, d), 0, one_x.at[stage, x])

    def turn(stage):
        if STAGES[stage][2]:
            for d in ahead:
                yy = wrap(y - d, NY)
                arrived(along_y(yy, x, stage, core), one_y.at[stage, yy])
            for d in reversed(near):
                push(along_y(every, x, stage, core), replica(0, d), 1, all_x.at[stage, x])
        for d in near:
            xx = wrap(x - d, NX)
            arrived(along_x(y, xx, stage, core), one_x.at[stage, xx])
        for d in reversed(ahead):
            push(along_x(y, every, stage, core), replica(d, 0), 2, all_y.at[stage, y])

    def finish(stage):
        for d in ahead:
            yy = wrap(y - d, NY)
            arrived(along_x(yy, every, stage, core), all_y.at[stage, yy])
        push(along_x(every, every, stage, core), sibling, 3, hand.at[stage, 1])
        if STAGES[stage][2]:
            for d in near:
                xx = wrap(x - d, NX)
                arrived(along_y(every, xx, stage, core), all_x.at[stage, xx])
            push(along_y(every, every, stage, core), sibling, 3, hand.at[stage, 0])

    def got(stage):
        arrived(along_x(every, every, stage, 1 - core), hand.at[stage, 1])
        if STAGES[stage][2]:
            arrived(along_y(every, every, stage, 1 - core), hand.at[stage, 0])

    lane = lax.broadcasted_iota(jnp.int32, (1, HD), 1)
    half = lax.rem(lane, HD // 2).astype(jnp.float32)
    frequency = jnp.exp(half * (-2.0 * math.log(ROPE_BASE) / HD))
    step = lax.broadcasted_iota(jnp.int32, (STEPS, HD), 0)
    n_rows = hidden.shape[0] // STEPS
    loads[4].wait()
    position = jnp.concatenate([step + len_ref[b] for b in range(n_rows)], axis=0)
    angle = position.astype(jnp.float32) * frequency
    cosine = jnp.cos(angle)
    sine = jnp.sin(angle) * jnp.where(lane < HD // 2, -1.0, 1.0)

    scale = 1.0 / math.sqrt(HD)
    n_att = query.shape[0]
    groups = query.shape[2] // HD

    def attend_cached(i):
        if i == 0:
            loads[0].wait()
            loads[1].wait()
        wide = query[i].astype(jnp.float32)
        q = jnp.concatenate([wide[:, g * HD : (g + 1) * HD] for g in range(groups)], axis=0)
        q = q.astype(jnp.bfloat16)
        s = lax.dot_general(q, cache[i, :, :HD], NT, preferred_element_type=jnp.float32) * scale
        place = lax.broadcasted_iota(jnp.int32, s.shape, 1)
        s = jnp.where(place < len_ref[parity * n_att + i], s, NEG)
        m = jnp.max(s, axis=1, keepdims=True)
        e = jnp.exp(s - m)
        here = pl.ds(i * groups * STEPS, groups * STEPS)
        q_out[here, :] = q
        peak_out[here, :] = jnp.broadcast_to(m, q.shape)
        total_out[here, :] = jnp.broadcast_to(jnp.sum(e, axis=1, keepdims=True), q.shape)
        sum_out[here, :] = jnp.dot(
            e.astype(jnp.bfloat16), cache[i, :, HD:], preferred_element_type=jnp.float32
        )

    def project(yy):
        wide = NX * 2 * block
        return jnp.dot(
            hidden[:, yy * wide : (yy + 1) * wide], cols[yy].reshape(wide, HD), preferred_element_type=jnp.float32
        )

    for i in range(n_att):
        attend_cached(i)
    loads[2].wait()

    def answer(first, end):
        for p in range(2 * first, 2 * end, 2):

            @pl.when(p > 2 * layer)
            def _():
                take(p)
                take(p + 1)
                give(p)
                give(p + 1)

    def meet(first, end):
        for p in range(2 * first, 2 * end, 2):

            @pl.when(p < 2 * layer)
            def _():
                take(p)
                take(p + 1)

            if p == 0:

                @pl.when(late)
                def _():
                    give(partner)

            @pl.when(p == 2 * layer)
            def _():
                take(partner)

    def hear():
        for p in range(2 * LATE, NTEN):
            take(p)

    def tell():
        for l in range(LATE, NTEN // 2):
            for r in plane:
                pl.semaphore_signal(
                    heard.at[l - LATE], inc=1, device_id=(r, ten), device_id_type=MESH
                )

    def confirm():
        for l in range(LATE, NTEN // 2):
            pl.semaphore_wait(heard.at[l - LATE], len(plane))
            give(2 * l)
            give(2 * l + 1)

    loads[3].wait()

    @pl.when(layer == 0)
    def _():
        answer(0, 3)
        meet(0, 3)
        begin(0)
        answer(3, 4)
        begin(1)
        turn(0)
        answer(4, LATE)
        hear()
        begin(2)
        tell()
        turn(1)
        confirm()
        turn(2)
        finish(0)
        finish(1)
        got(0)
        got(1)
        finish(2)
        got(2)

    @pl.when((layer > 0) & (layer < 3))
    def _():
        answer(0, 4)
        meet(0, 4)
        begin(3)
        answer(4, 8)
        begin(4)
        turn(3)
        turn(4)
        finish(3)
        got(3)
        finish(4)
        got(4)

    @pl.when(layer >= 3)
    def _():
        answer(3, 8)
        meet(0, 4)
        begin(3)
        meet(4, 8)
        begin(4)
        turn(3)
        turn(4)
        finish(3)
        got(3)
        finish(4)
        got(4)

    projected = project(0)
    for yy in range(1, NY):
        projected += project(yy)

    loads[5].wait()
    whole = projected + bias_ref[...].astype(jnp.float32)
    rotated = whole * cosine + pltpu.roll(whole, HD // 2, 1) * sine
    whole = jnp.where(parity == 0, rotated, whole).astype(jnp.bfloat16)
    n_half = whole.shape[0] // 2
    mine[0] = whole[:n_half]
    mine[1] = whole[n_half:]
    exchange = pltpu.make_async_remote_copy(
        src_ref=mine.at[1 - parity], dst_ref=other, send_sem=pair_send, recv_sem=pair_recv,
        device_id=(rep, partner), device_id_type=MESH,
    )
    exchange.start()
    exchange.wait()
    kept, theirs = mine[parity], other[...]
    new_keys = jnp.where(parity == 0, kept, theirs)
    new_values = jnp.where(parity == 0, theirs, kept)

    keys[...] = new_keys
    values[...] = new_values

    given = parts.at[pl.ds(0, NTEN - 1)]
    pltpu.make_async_copy(given, given, part_send).wait()
    for kind, ref in enumerate(
        (
            cols.at[0, pl.ds(0, (NX + NY - 2) // 2), 0],
            cols.at[pl.ds(0, NY // 2), pl.ds(0, NX - 1), 0],
            cols.at[pl.ds(0, NY - 1), pl.ds(0, NX // 2), 0],
            cols.at[pl.ds(0, NY // 2)],
        )
    ):
        pltpu.make_async_copy(ref, ref, send.at[kind]).wait()


def join(
    STEPS,
    cols, q_ref, peak_ref, total_ref, sum_ref, keys, values,
    cols_out, att_out,
    att, sems,
):
    out = pltpu.make_async_copy(cols, cols_out, sems.at[0])
    out.start()
    scale = 1.0 / math.sqrt(HD)
    n_att, _, wide = att.shape
    groups = wide // HD
    s = lax.dot_general(q_ref[...], keys[...], NT, preferred_element_type=jnp.float32) * scale
    of_query = lax.broadcasted_iota(jnp.int32, s.shape, 0)
    of_key = lax.broadcasted_iota(jnp.int32, s.shape, 1)
    same_row = lax.div(of_query, groups * STEPS) == lax.div(of_key, STEPS)
    causal = lax.rem(of_key, STEPS) <= lax.rem(of_query, STEPS)
    s = jnp.where(same_row & causal, s, NEG)
    old_peak = peak_ref[...]
    peak = jnp.maximum(old_peak, jnp.max(s, axis=1, keepdims=True))
    e = jnp.exp(s - peak[:, : s.shape[1]])
    shrink = jnp.exp(old_peak - peak)
    total = total_ref[...] * shrink + jnp.sum(e, axis=1, keepdims=True)
    mixed = sum_ref[...] * shrink
    mixed += jnp.dot(e.astype(jnp.bfloat16), values[...], preferred_element_type=jnp.float32)
    mixed = mixed / total
    for i in range(n_att):
        base = i * groups * STEPS
        att[i] = jnp.concatenate(
            [mixed[base + g * STEPS : base + (g + 1) * STEPS] for g in range(groups)], axis=1
        ).astype(jnp.bfloat16)
    done = pltpu.make_async_copy(att, att_out, sems.at[1])
    done.start()
    done.wait()
    out.wait()


def solution(mesh):
    n_rep, n_ten = mesh.shape["replica"], mesh.shape["tensor"]
    NX = 8
    NY = n_rep // (2 * NX)

    def per_device(hidden_rows, prior_bias, cache_blocks, queries, cache_lengths, updated_rows):
        n_rows, steps, width = hidden_rows.shape
        piece = updated_rows.shape[0]
        vmem = pl.BlockSpec(memory_space=pltpu.VMEM)
        block = n_ten * piece
        n_att, _, q_width = queries.shape[1:]
        n_query = n_att * steps * (q_width // HD)
        half = n_rows * steps // 2
        gathered = pl.pallas_call(
            functools.partial(kernel, NY, NX, n_ten, piece, steps),
            out_shape=(
                jax.ShapeDtypeStruct((NY, NX, 2, block, HD), jnp.bfloat16),
                jax.ShapeDtypeStruct((n_query, HD), jnp.bfloat16),
                *[jax.ShapeDtypeStruct((n_query, HD), jnp.float32)] * 3,
                *[jax.ShapeDtypeStruct((half, HD), jnp.bfloat16)] * 2,
            ),
            in_specs=[pl.BlockSpec(memory_space=pltpu.HBM)] * 6,
            out_specs=(vmem,) * 7,
            scratch_shapes=[
                pltpu.VMEM((n_ten, piece, HD), jnp.bfloat16),
                pltpu.VMEM((n_rows * steps, width), jnp.bfloat16),
                pltpu.VMEM(cache_blocks.shape[1:], jnp.bfloat16),
                pltpu.VMEM(queries.shape[1:], jnp.bfloat16),
                pltpu.VMEM((1, HD), jnp.bfloat16),
                pltpu.SMEM((n_rows,), jnp.int32),
                pltpu.VMEM((2, n_rows * steps // 2, HD), jnp.bfloat16),
                pltpu.VMEM((n_rows * steps // 2, HD), jnp.bfloat16),
                pltpu.SemaphoreType.DMA,
                pltpu.SemaphoreType.DMA((n_ten,)),
                pltpu.SemaphoreType.DMA((4,)),
                *[pltpu.SemaphoreType.DMA((len(STAGES), n)) for n in (NY, NX, NY, NX, 2)],
                pltpu.SemaphoreType.REGULAR((n_ten // 2 - LATE,)),
                pltpu.SemaphoreType.DMA((6,)),
                pltpu.SemaphoreType.DMA,
                pltpu.SemaphoreType.DMA,
            ],
            compiler_params=pltpu.CompilerParams(
                collective_id=0, has_side_effects=True, vmem_limit_bytes=40 << 20
            ),
        )(
            *(
                pltpu.with_memory_space_constraint(a, pltpu.HBM)
                for a in (
                    updated_rows,
                    hidden_rows.reshape(n_rows * steps, width),
                    cache_blocks[0],
                    queries[0],
                    prior_bias.reshape(1, HD),
                    cache_lengths,
                )
            )
        )
        columns, attended = pl.pallas_call(
            functools.partial(join, steps),
            out_shape=(
                jax.ShapeDtypeStruct(gathered[0].shape, jnp.bfloat16),
                jax.ShapeDtypeStruct(queries.shape[1:], jnp.bfloat16),
            ),
            in_specs=[pl.BlockSpec(memory_space=pl.ANY)] + [vmem] * 6,
            out_specs=(pl.BlockSpec(memory_space=pltpu.HBM),) * 2,
            scratch_shapes=[
                pltpu.VMEM(queries.shape[1:], jnp.bfloat16),
                pltpu.SemaphoreType.DMA((2,)),
            ],
            compiler_params=pltpu.CompilerParams(vmem_limit_bytes=16 << 20),
        )(*gathered)
        return attended[None], columns.reshape(n_rep * block, HD)

    return jax.shard_map(
        per_device,
        mesh=mesh,
        in_specs=(
            P("replica", None, None),
            P("tensor"),
            P("tensor", "replica", None, None),
            P("tensor", "replica", None, None),
            P("replica"),
            P(("replica", "tensor"), None),
        ),
        out_specs=(P("tensor", "replica", None, None), P(None, "tensor")),
        check_vma=False,
    )
```

```python
import functools
import math

import jax
import jax.numpy as jnp
from jax import lax
from jax.experimental import pallas as pl
from jax.experimental.pallas import tpu as pltpu
from jax.sharding import PartitionSpec as P

ROPE_BASE = 1000000.0
HD = 128
NEG = -1e30
MESH = pl.DeviceIdType.MESH
NT = (((1,), (1,)), ((), ()))
LATE = 6
STAGES = ((0, 3, 2), (3, 1, 0), (4, 4, 2), (0, 4, 2), (4, 4, 2))


def kernel(
    NY, NX, NTEN, PIECE, STEPS,
    rows_hbm, hidden_hbm, cache_hbm, query_hbm, bias_hbm, len_hbm,
    cols, q_out, peak_out, total_out, sum_out, keys, values,
    parts, hidden, cache, query, bias_ref, len_ref, mine, other,
    part_send, part_recv, send, one_y, one_x, all_y, all_x, hand, heard, load, pair_send, pair_recv,
):
    rep = lax.axis_index("replica")
    ten = lax.axis_index("tensor")
    core = lax.rem(rep, 2)
    chip = lax.div(rep, 2)
    x = lax.rem(chip, NX)
    y = lax.div(chip, NX)
    parity = lax.rem(ten, 2)
    block = NTEN * PIECE

    def replica(dy, dx, c=None):
        yy = lax.rem(y + dy + 2 * NY, NY)
        xx = lax.rem(x + dx + 2 * NX, NX)
        return (yy * NX + xx) * 2 + (core if c is None else c)

    def wrap(i, n):
        return lax.rem(i + 2 * n, n)

    sibling = replica(0, 0, 1 - core)
    near = sorted(range(1 - NX // 2, NX // 2 + 1), key=abs)[1:]
    ahead = sorted(range(1 - NY // 2, NY // 2 + 1), key=abs)[1:]
    layer = lax.div(ten, 2)
    partner = ten + 1 - 2 * parity

    barrier = pltpu.get_barrier_semaphore()
    late = layer >= LATE
    plane = [replica(0, d) for d in near] + [replica(d, 0) for d in ahead] + [sibling]

    @pl.when(jnp.logical_not(late))
    def _():
        for r in plane:
            pl.semaphore_signal(barrier, inc=1, device_id=(r, ten), device_id_type=MESH)
        pl.semaphore_signal(barrier, inc=1, device_id=(rep, partner), device_id_type=MESH)

    for p in reversed(range(2, NTEN)):

        @pl.when(p >= 2 * layer + 2)
        def _():
            pl.semaphore_signal(barrier, inc=1, device_id=(rep, p), device_id_type=MESH)

    loads = [
        pltpu.make_async_copy(query_hbm, query, load.at[0]),
        pltpu.make_async_copy(cache_hbm, cache, load.at[1]),
        pltpu.make_async_copy(hidden_hbm, hidden, load.at[2]),
        pltpu.make_async_copy(
            rows_hbm.at[:, pl.ds(pl.multiple_of(ten * HD, HD), HD)], parts.at[ten], load.at[3]
        ),
        pltpu.make_async_copy(len_hbm, len_ref, load.at[4]),
        pltpu.make_async_copy(bias_hbm, bias_ref, load.at[5]),
    ]
    for i in (3, 4, 5, 0, 1, 2):
        loads[i].start()
    @pl.when(late)
    def _():
        pl.semaphore_wait(barrier, 2 * layer)

    @pl.when(jnp.logical_not(late))
    def _():
        pl.semaphore_wait(barrier, len(plane) + 2 * layer + 1)

    def give(p):
        pltpu.make_async_remote_copy(
            src_ref=rows_hbm.at[:, pl.ds(pl.multiple_of(p * HD, HD), HD)], dst_ref=parts.at[ten],
            send_sem=part_send, recv_sem=part_recv.at[ten],
            device_id=(rep, p), device_id_type=MESH,
        ).start()

    def take(p):
        pltpu.make_async_copy(parts.at[p], parts.at[p], part_recv.at[p]).wait()

    for p in range(NTEN - 2):

        @pl.when(p < 2 * layer)
        def _():
            give(p)

    @pl.when(jnp.logical_not(late))
    def _():
        give(partner)

    unit = 2 * PIECE

    def along_y(yy_or_all, xx, stage, c):
        first, _, part = STAGES[stage]
        return cols.at[yy_or_all, xx, c, pl.ds(first * unit, part * unit), :]

    def along_x(yy, xx_or_all, stage, c):
        first, n, part = STAGES[stage]
        return cols.at[yy, xx_or_all, c, pl.ds((first + part) * unit, (n - part) * unit), :]

    def push(ref, to, kind, recv_sem):
        pltpu.make_async_remote_copy(
            src_ref=ref, dst_ref=ref, send_sem=send.at[kind], recv_sem=recv_sem,
            device_id=(to, ten), device_id_type=MESH,
        ).start()

    def arrived(ref, recv_sem):
        pltpu.make_async_copy(ref, ref, recv_sem).wait()

    every = slice(None)

    def begin(stage):
        first, n, part = STAGES[stage]
        pieces = [parts[p].astype(jnp.float32) for p in range(2 * first, 2 * (first + n))]
        cols[y, x, core, pl.ds(first * unit, n * unit), :] = jnp.concatenate(
            pieces, axis=0
        ).astype(jnp.bfloat16)
        if part:
            for d in reversed(ahead):
                push(along_y(y, x, stage, core), replica(d, 0), 0, one_y.at[stage, y])
        for d in reversed(near):
            push(along_x(y, x, stage, core), replica(0, d), 0, one_x.at[stage, x])

    def turn_y(stage):
        if STAGES[stage][2]:
            for d in ahead:
                yy = wrap(y - d, NY)
                arrived(along_y(yy, x, stage, core), one_y.at[stage, yy])
            for d in reversed(near):
                push(along_y(every, x, stage, core), replica(0, d), 1, all_x.at[stage, x])

    def turn_x(stage):
        for d in near:
            xx = wrap(x - d, NX)
            arrived(along_x(y, xx, stage, core), one_x.at[stage, xx])
        for d in reversed(ahead):
            push(along_x(y, every, stage, core), replica(d, 0), 2, all_y.at[stage, y])

    def turn(stage):
        turn_y(stage)
        turn_x(stage)

    def finish(stage):
        for d in ahead:
            yy = wrap(y - d, NY)
            arrived(along_x(yy, every, stage, core), all_y.at[stage, yy])
        push(along_x(every, every, stage, core), sibling, 3, hand.at[stage, 1])
        if STAGES[stage][2]:
            for d in near:
                xx = wrap(x - d, NX)
                arrived(along_y(every, xx, stage, core), all_x.at[stage, xx])
            push(along_y(every, every, stage, core), sibling, 3, hand.at[stage, 0])

    def got(stage):
        arrived(along_x(every, every, stage, 1 - core), hand.at[stage, 1])
        if STAGES[stage][2]:
            arrived(along_y(every, every, stage, 1 - core), hand.at[stage, 0])

    lane = lax.broadcasted_iota(jnp.int32, (1, HD), 1)
    half = lax.rem(lane, HD // 2).astype(jnp.float32)
    frequency = jnp.exp(half * (-2.0 * math.log(ROPE_BASE) / HD))
    step = lax.broadcasted_iota(jnp.int32, (STEPS, HD), 0)
    n_rows = hidden.shape[0] // STEPS
    loads[4].wait()
    position = jnp.concatenate([step + len_ref[b] for b in range(n_rows)], axis=0)
    angle = position.astype(jnp.float32) * frequency
    cosine = jnp.cos(angle)
    sine = jnp.sin(angle) * jnp.where(lane < HD // 2, -1.0, 1.0)

    scale = 1.0 / math.sqrt(HD)
    n_att = query.shape[0]
    groups = query.shape[2] // HD

    def attend_cached(i):
        if i == 0:
            loads[0].wait()
            loads[1].wait()
        wide = query[i].astype(jnp.float32)
        q = jnp.concatenate([wide[:, g * HD : (g + 1) * HD] for g in range(groups)], axis=0)
        q = q.astype(jnp.bfloat16)
        s = lax.dot_general(q, cache[i, :, :HD], NT, preferred_element_type=jnp.float32) * scale
        place = lax.broadcasted_iota(jnp.int32, s.shape, 1)
        s = jnp.where(place < len_ref[parity * n_att + i], s, NEG)
        m = jnp.max(s, axis=1, keepdims=True)
        e = jnp.exp(s - m)
        here = pl.ds(i * groups * STEPS, groups * STEPS)
        q_out[here, :] = q
        peak_out[here, :] = jnp.broadcast_to(m, q.shape)
        total_out[here, :] = jnp.broadcast_to(jnp.sum(e, axis=1, keepdims=True), q.shape)
        sum_out[here, :] = jnp.dot(
            e.astype(jnp.bfloat16), cache[i, :, HD:], preferred_element_type=jnp.float32
        )

    def project(yy):
        wide = NX * 2 * block
        return jnp.dot(
            hidden[:, yy * wide : (yy + 1) * wide], cols[yy].reshape(wide, HD), preferred_element_type=jnp.float32
        )

    for i in range(n_att):
        attend_cached(i)
    loads[2].wait()

    def answer(first, end):
        for p in range(2 * first, 2 * end, 2):

            @pl.when(p > 2 * layer)
            def _():
                take(p)
                take(p + 1)
                give(p)
                give(p + 1)

    def meet(first, end):
        for p in range(2 * first, 2 * end, 2):

            @pl.when(p < 2 * layer)
            def _():
                take(p)
                take(p + 1)

            if p == 0:

                @pl.when(late)
                def _():
                    give(partner)

            @pl.when(p == 2 * layer)
            def _():
                take(partner)

    def hear():
        for p in range(2 * LATE, NTEN):
            take(p)

    def tell():
        for l in range(LATE, NTEN // 2):
            for r in plane:
                pl.semaphore_signal(
                    heard.at[l - LATE], inc=1, device_id=(r, ten), device_id_type=MESH
                )

    def confirm():
        for l in range(LATE, NTEN // 2):
            pl.semaphore_wait(heard.at[l - LATE], len(plane))
            give(2 * l)
            give(2 * l + 1)

    loads[3].wait()

    @pl.when(layer == 0)
    def _():
        answer(0, 3)
        meet(0, 3)
        begin(0)
        answer(3, 4)
        begin(1)
        turn(0)
        answer(4, LATE)
        hear()
        begin(2)
        tell()
        turn(1)
        turn_y(2)
        confirm()
        turn_x(2)
        finish(0)
        finish(1)
        got(0)
        got(1)
        finish(2)
        got(2)

    @pl.when((layer > 0) & (layer < 3))
    def _():
        answer(0, 4)
        meet(0, 4)
        begin(3)
        answer(4, 8)
        begin(4)
        turn(3)
        turn(4)
        finish(3)
        got(3)
        finish(4)
        got(4)

    @pl.when(layer >= 3)
    def _():
        answer(3, 8)
        meet(0, 4)
        begin(3)
        meet(4, 8)
        begin(4)
        turn(3)
        turn(4)
        finish(3)
        got(3)
        finish(4)
        got(4)

    projected = project(0)
    for yy in range(1, NY):
        projected += project(yy)

    loads[5].wait()
    whole = projected + bias_ref[...].astype(jnp.float32)
    rotated = whole * cosine + pltpu.roll(whole, HD // 2, 1) * sine
    whole = jnp.where(parity == 0, rotated, whole).astype(jnp.bfloat16)
    n_half = whole.shape[0] // 2
    mine[0] = whole[:n_half]
    mine[1] = whole[n_half:]
    exchange = pltpu.make_async_remote_copy(
        src_ref=mine.at[1 - parity], dst_ref=other, send_sem=pair_send, recv_sem=pair_recv,
        device_id=(rep, partner), device_id_type=MESH,
    )
    exchange.start()
    exchange.wait()
    kept, theirs = mine[parity], other[...]
    new_keys = jnp.where(parity == 0, kept, theirs)
    new_values = jnp.where(parity == 0, theirs, kept)

    keys[...] = new_keys
    values[...] = new_values

    given = parts.at[pl.ds(0, NTEN - 1)]
    pltpu.make_async_copy(given, given, part_send).wait()
    for kind, ref in enumerate(
        (
            cols.at[0, pl.ds(0, (NX + NY - 2) // 2), 0],
            cols.at[pl.ds(0, NY // 2), pl.ds(0, NX - 1), 0],
            cols.at[pl.ds(0, NY - 1), pl.ds(0, NX // 2), 0],
            cols.at[pl.ds(0, NY // 2)],
        )
    ):
        pltpu.make_async_copy(ref, ref, send.at[kind]).wait()


def join(
    STEPS,
    cols, q_ref, peak_ref, total_ref, sum_ref, keys, values,
    cols_out, att_out,
    att, sems,
):
    out = pltpu.make_async_copy(cols, cols_out, sems.at[0])
    out.start()
    scale = 1.0 / math.sqrt(HD)
    n_att, _, wide = att.shape
    groups = wide // HD
    s = lax.dot_general(q_ref[...], keys[...], NT, preferred_element_type=jnp.float32) * scale
    of_query = lax.broadcasted_iota(jnp.int32, s.shape, 0)
    of_key = lax.broadcasted_iota(jnp.int32, s.shape, 1)
    same_row = lax.div(of_query, groups * STEPS) == lax.div(of_key, STEPS)
    causal = lax.rem(of_key, STEPS) <= lax.rem(of_query, STEPS)
    s = jnp.where(same_row & causal, s, NEG)
    old_peak = peak_ref[...]
    peak = jnp.maximum(old_peak, jnp.max(s, axis=1, keepdims=True))
    e = jnp.exp(s - peak[:, : s.shape[1]])
    shrink = jnp.exp(old_peak - peak)
    total = total_ref[...] * shrink + jnp.sum(e, axis=1, keepdims=True)
    mixed = sum_ref[...] * shrink
    mixed += jnp.dot(e.astype(jnp.bfloat16), values[...], preferred_element_type=jnp.float32)
    mixed = mixed / total
    for i in range(n_att):
        base = i * groups * STEPS
        att[i] = jnp.concatenate(
            [mixed[base + g * STEPS : base + (g + 1) * STEPS] for g in range(groups)], axis=1
        ).astype(jnp.bfloat16)
    done = pltpu.make_async_copy(att, att_out, sems.at[1])
    done.start()
    done.wait()
    out.wait()


def solution(mesh):
    n_rep, n_ten = mesh.shape["replica"], mesh.shape["tensor"]
    NX = 8
    NY = n_rep // (2 * NX)

    def per_device(hidden_rows, prior_bias, cache_blocks, queries, cache_lengths, updated_rows):
        n_rows, steps, width = hidden_rows.shape
        piece = updated_rows.shape[0]
        vmem = pl.BlockSpec(memory_space=pltpu.VMEM)
        block = n_ten * piece
        n_att, _, q_width = queries.shape[1:]
        n_query = n_att * steps * (q_width // HD)
        half = n_rows * steps // 2
        gathered = pl.pallas_call(
            functools.partial(kernel, NY, NX, n_ten, piece, steps),
            out_shape=(
                jax.ShapeDtypeStruct((NY, NX, 2, block, HD), jnp.bfloat16),
                jax.ShapeDtypeStruct((n_query, HD), jnp.bfloat16),
                *[jax.ShapeDtypeStruct((n_query, HD), jnp.float32)] * 3,
                *[jax.ShapeDtypeStruct((half, HD), jnp.bfloat16)] * 2,
            ),
            in_specs=[pl.BlockSpec(memory_space=pltpu.HBM)] * 6,
            out_specs=(vmem,) * 7,
            scratch_shapes=[
                pltpu.VMEM((n_ten, piece, HD), jnp.bfloat16),
                pltpu.VMEM((n_rows * steps, width), jnp.bfloat16),
                pltpu.VMEM(cache_blocks.shape[1:], jnp.bfloat16),
                pltpu.VMEM(queries.shape[1:], jnp.bfloat16),
                pltpu.VMEM((1, HD), jnp.bfloat16),
                pltpu.SMEM((n_rows,), jnp.int32),
                pltpu.VMEM((2, n_rows * steps // 2, HD), jnp.bfloat16),
                pltpu.VMEM((n_rows * steps // 2, HD), jnp.bfloat16),
                pltpu.SemaphoreType.DMA,
                pltpu.SemaphoreType.DMA((n_ten,)),
                pltpu.SemaphoreType.DMA((4,)),
                *[pltpu.SemaphoreType.DMA((len(STAGES), n)) for n in (NY, NX, NY, NX, 2)],
                pltpu.SemaphoreType.REGULAR((n_ten // 2 - LATE,)),
                pltpu.SemaphoreType.DMA((6,)),
                pltpu.SemaphoreType.DMA,
                pltpu.SemaphoreType.DMA,
            ],
            compiler_params=pltpu.CompilerParams(
                collective_id=0, has_side_effects=True, vmem_limit_bytes=40 << 20
            ),
        )(
            *(
                pltpu.with_memory_space_constraint(a, pltpu.HBM)
                for a in (
                    updated_rows,
                    hidden_rows.reshape(n_rows * steps, width),
                    cache_blocks[0],
                    queries[0],
                    prior_bias.reshape(1, HD),
                    cache_lengths,
                )
            )
        )
        columns, attended = pl.pallas_call(
            functools.partial(join, steps),
            out_shape=(
                jax.ShapeDtypeStruct(gathered[0].shape, jnp.bfloat16),
                jax.ShapeDtypeStruct(queries.shape[1:], jnp.bfloat16),
            ),
            in_specs=[pl.BlockSpec(memory_space=pl.ANY)] + [vmem] * 6,
            out_specs=(pl.BlockSpec(memory_space=pltpu.HBM),) * 2,
            scratch_shapes=[
                pltpu.VMEM(queries.shape[1:], jnp.bfloat16),
                pltpu.SemaphoreType.DMA((2,)),
            ],
            compiler_params=pltpu.CompilerParams(vmem_limit_bytes=16 << 20),
        )(*gathered)
        return attended[None], columns.reshape(n_rep * block, HD)

    return jax.shard_map(
        per_device,
        mesh=mesh,
        in_specs=(
            P("replica", None, None),
            P("tensor"),
            P("tensor", "replica", None, None),
            P("tensor", "replica", None, None),
            P("replica"),
            P(("replica", "tensor"), None),
        ),
        out_specs=(P("tensor", "replica", None, None), P(None, "tensor")),
        check_vma=False,
    )
```
